128 devices in a mesh: width: 8 (over y_lo, z), hidden: 16 (over x, y_hi, core).
Axes of the slice: x: 4, y: 4 (y_hi: 2, y_lo: 2; y = y_hi * 2 + y_lo), z: 4, core: 2. Of those that a mesh axis runs over, the one named last changes fastest.
Arguments:
- tokens: bfloat16 [768, 8192], P('hidden', 'width'), may hold values from -6 to 6
- gate_weight: bfloat16 [8192, 28672], P('width', 'hidden'), may hold values from -0.09375 to 0.09375
- up_weight: bfloat16 [8192, 28672], P('width', 'hidden'), may hold values from -0.09375 to 0.09375
- down_weight: bfloat16 [28672, 8192], P('hidden', 'width'), may hold values from -0.046875 to 0.046875
- grad_out: bfloat16 [768, 8192], P('hidden', 'width'), may hold values from -6 to 6
- pattern_gate: int32 [64, 112], P('width'), may hold values from 0 to 223, all different within a row
- pattern_up: int32 [64, 112], P('width'), may hold values from 0 to 223, all different within a row
- pattern_down: int32 [224, 32], P('hidden'), may hold values from 0 to 63, all different within a row
Outputs:
- output: bfloat16 [768, 8192], P('hidden', 'width')
- grad_tokens: bfloat16 [768, 8192], P('hidden', 'width')
- grad_gate: bfloat16 [8192, 28672], P('width', 'hidden')
- grad_up: bfloat16 [8192, 28672], P('width', 'hidden')
- grad_down: bfloat16 [28672, 8192], P('hidden', 'width')
The draws below stay inside these ranges and needn't reach their ends.
Inputs may be any that keep to these rules, and one draw needn't show every extreme that they name: `pattern_gate`: each row names 112 distinct block columns, and every block column is named by some row. `pattern_up`: each row names 112 distinct block columns, and every block column is named by some row. `pattern_down`: each row names 32 distinct block columns, and every block column is named by some row.
All inputs are finite; a program needn't handle non-finite values.
Results may differ from the reference program's by a relative error of at most 0.005.
Values may be sent and summed in bfloat16 or wider, within the bound.
A program may use at most 128 MiB of HBM per device.

```python
import jax
import jax.numpy as jnp
from jax import lax

D = 8192
FF = 28672
BLOCK = 128
TOKENS = 768
KEEP_IN = 112
KEEP_OUT = 32


def block_scale(own_key, dims, shards, least, largest):
    factor_of = 1.0
    for axis_at, shards_of in shards:
        heights = jax.random.uniform(jax.random.fold_in(jax.random.fold_in(own_key, 6), axis_at), (shards_of,), jnp.float32, least / len(shards), largest / len(shards))
        factor_of = factor_of * jnp.repeat(jnp.exp(heights), dims[axis_at] // shards_of).reshape((-1,) + (1,) * (len(dims) - 1 - axis_at))
    return factor_of


def distinct(own_key, rows, number_of, top, lift):
    ranking = jax.random.permutation(jax.random.fold_in(own_key, 1), number_of)
    boost = ranking
    for power in range(3):
        boost = boost * boost // number_of
    boost = boost * lift // number_of
    tickets = jax.random.randint(jax.random.fold_in(own_key, 2), (rows, number_of), 0, 4096) + boost
    sure = jax.random.permutation(jax.random.fold_in(own_key, 3), rows)[jnp.arange(number_of) % rows]
    tickets = jnp.where(jnp.arange(rows)[:, None] == sure[None, :], 1 << 14, tickets)
    score = tickets * number_of + jnp.arange(number_of)
    return lax.top_k(score.astype(jnp.int32), top)[1].astype(jnp.int32)


def noise(stream_key, extent, deviation, most, pieces=(), held_as=jnp.bfloat16):
    drawn = jax.random.normal(stream_key, extent, jnp.float32) * deviation
    if len(pieces) > 0:
        drawn = block_scale(stream_key, extent, pieces, -0.22, 0.18) * drawn
    return jnp.clip(drawn, min=-most, max=most).astype(held_as)


def setup_inputs(seed: int = 0) -> dict:
    arg_keys = jax.random.split(jax.random.key(seed), 9)
    return {
        "tokens": noise(arg_keys[0], (TOKENS, D), 1.0, 6.0, ((0, 16), (1, 8))),
        "gate_weight": noise(arg_keys[1], (D, FF), (D // 2) ** -0.5, 0.09375, ((0, 8), (1, 16))),
        "up_weight": noise(arg_keys[2], (D, FF), (D // 2) ** -0.5, 0.09375, ((0, 8), (1, 16))),
        "down_weight": noise(arg_keys[3], (FF, D), (FF // 2) ** -0.5, 0.046875, ((0, 16), (1, 8))),
        "grad_out": noise(arg_keys[4], (TOKENS, D), 1.0, 6.0, ((0, 16), (1, 8))),
        "pattern_gate": distinct(arg_keys[5], (D // BLOCK), FF // BLOCK, KEEP_IN, 0),
        "pattern_up": distinct(arg_keys[6], (D // BLOCK), FF // BLOCK, KEEP_IN, 0),
        "pattern_down": distinct(arg_keys[7], (FF // BLOCK), D // BLOCK, KEEP_OUT, 0),
    }


def block_mask(pattern, count):
    columns = jnp.arange(count, dtype=jnp.int32)
    hit = jnp.any(pattern[:, :, None] == columns[None, None, :], axis=1)
    return jnp.repeat(jnp.repeat(hit, BLOCK, axis=0), BLOCK, axis=1)


def reference(tokens, gate_weight, up_weight, down_weight, grad_out, pattern_gate, pattern_up, pattern_down):
    zero = jnp.zeros((), jnp.bfloat16)
    mask_gate = block_mask(pattern_gate, FF // BLOCK)
    mask_up = block_mask(pattern_up, FF // BLOCK)
    mask_down = block_mask(pattern_down, D // BLOCK)
    w_gate = jnp.where(mask_gate, gate_weight, zero)
    w_up = jnp.where(mask_up, up_weight, zero)
    w_down = jnp.where(mask_down, down_weight, zero)
    gate = jnp.dot(tokens, w_gate, preferred_element_type=jnp.float32)
    up = jnp.dot(tokens, w_up, preferred_element_type=jnp.float32)
    sig = jax.nn.sigmoid(gate)
    hidden = (gate * sig * up).astype(jnp.bfloat16)
    output = jnp.dot(hidden, w_down, preferred_element_type=jnp.float32).astype(jnp.bfloat16)
    grad_hidden = lax.dot_general(grad_out, w_down, (((1,), (1,)), ((), ())), preferred_element_type=jnp.float32)
    d_gate = (grad_hidden * up * sig * (1.0 + gate * (1.0 - sig))).astype(jnp.bfloat16)
    d_up = (grad_hidden * gate * sig).astype(jnp.bfloat16)
    contract = (((0,), (0,)), ((), ()))
    grad_down = jnp.where(mask_down, lax.dot_general(hidden, grad_out, contract, preferred_element_type=jnp.float32), 0.0).astype(jnp.bfloat16)
    grad_gate = jnp.where(mask_gate, lax.dot_general(tokens, d_gate, contract, preferred_element_type=jnp.float32), 0.0).astype(jnp.bfloat16)
    grad_up = jnp.where(mask_up, lax.dot_general(tokens, d_up, contract, preferred_element_type=jnp.float32), 0.0).astype(jnp.bfloat16)
    back = (((1,), (1,)), ((), ()))
    grad_tokens = lax.dot_general(d_gate, w_gate, back, preferred_element_type=jnp.float32)
    grad_tokens = grad_tokens + lax.dot_general(d_up, w_up, back, preferred_element_type=jnp.float32)
    return output, grad_tokens.astype(jnp.bfloat16), grad_gate, grad_up, grad_down
```

```python
import functools

import jax
import jax.numpy as jnp
from jax import lax
from jax.experimental import pallas as pl
from jax.experimental.pallas import tpu as pltpu
from jax.sharding import PartitionSpec as P

BLOCK = 128
COLS = 256
MESH = pl.DeviceIdType.MESH
F32 = jnp.float32
BF16 = jnp.bfloat16


def remote(src, dst, send, recv, device):
    return pltpu.make_async_remote_copy(
        src_ref=src, dst_ref=dst, send_sem=send, recv_sem=recv,
        device_id=device, device_id_type=MESH,
    )


def nt(a, b):
    return lax.dot_general(a, b, (((1,), (1,)), ((), ())), preferred_element_type=F32)


def layer_kernel(
    nk,
    tokens, gate_w, up_w, down_w, grad_out, pat_gate, pat_up, pat_down,
    output, grad_tokens, act_out, tok_out, grd_out,
    wg, wu, wd, mg, mu, md, tok, grd, own, ysend, yrecv, zsend, zrecv, ag, acc,
    csend, crecv, tsend, trecv, first,
    w_sem, o_sem, hs_sem, hr_sem, hf_sem, ys_sem, yr_sem, zs_sem, zr_sem,
    as_sem, ar_sem, cs_sem, cr_sem, ts_sem, tr_sem, act_sem, all_sem,
):
    steps = 2 * nk
    width = lax.axis_index("width")
    hid = lax.axis_index("hidden")
    z = lax.rem(width, 4)
    yl = lax.div(width, 4)
    core = lax.rem(hid, 2)
    chip = lax.div(hid, 2)
    zp, zm, zq = lax.rem(z + 1, 4), lax.rem(z + 3, 4), lax.rem(z + 2, 4)

    def at_z(to):
        return (yl * 4 + to, hid)

    partner = ((1 - yl) * 4 + z, hid)
    sibling = (width, chip * 2 + 1 - core)

    def at_chip(to, its_core):
        return (width, to * 2 + its_core)

    def place(j):
        return lax.rem(j + 4 * yl, 8)

    mine = place(chip)

    def weight_copies(k):
        cols = pl.ds(k * COLS, COLS) if isinstance(k, int) else pl.ds(pl.multiple_of(k * COLS, COLS), COLS)
        return (
            pltpu.make_async_copy(gate_w.at[:, cols], wg.at[k], w_sem.at[0, k]),
            pltpu.make_async_copy(up_w.at[:, cols], wu.at[k], w_sem.at[1, k]),
            pltpu.make_async_copy(down_w.at[cols, :], wd.at[k], w_sem.at[2, k]),
        )

    own_copies = (
        pltpu.make_async_copy(tokens, tok.at[core, mine], o_sem.at[0]),
        pltpu.make_async_copy(grad_out, grd.at[core, mine], o_sem.at[1]),
    )
    for copy in own_copies:
        copy.start()
    for k in range(nk):
        for copy in weight_copies(k):
            copy.start()

    barrier = pltpu.get_barrier_semaphore()
    for to in (zp, zm, zq):
        pl.semaphore_signal(barrier, inc=1, device_id=at_z(to), device_id_type=MESH)
    pl.semaphore_signal(barrier, inc=1, device_id=partner, device_id_type=MESH)
    pl.semaphore_signal(barrier, inc=1, device_id=sibling, device_id_type=MESH)
    for d in range(1, 8):
        for c in range(2):
            pl.semaphore_signal(
                barrier, inc=1, device_id=at_chip(lax.rem(chip + d, 8), c), device_id_type=MESH
            )
    pl.semaphore_wait(barrier, 19)

    pair = ((tokens, tok), (grad_out, grd))

    def gather_send(c):
        @pl.when(core == c)
        def _():
            for a, (src, dst) in enumerate(pair):
                def send(d, carry):
                    remote(src, dst.at[c, mine], hs_sem.at[a, d], hr_sem.at[c, a, d],
                           at_chip(lax.rem(chip + d, 8), c)).start()
                    return carry
                lax.fori_loop(1, 8, send, 0)
                remote(src, dst.at[c, mine], hs_sem.at[a, 0], hr_sem.at[c, a, 0], sibling).start()

    def arrived(c, a, d):
        dst = pair[a][1].at[c, place(lax.rem(chip + 8 - d, 8))]
        remote(dst, dst, hs_sem.at[a, d], hr_sem.at[c, a, d], sibling).wait_recv()
        return dst

    def gather_forward(c, a):
        @pl.when(core == c)
        def _():
            def hand_on(d, carry):
                dst = arrived(c, a, d)
                remote(dst, dst, hf_sem.at[a, d], hr_sem.at[c, a, d], sibling).start()
                return carry
            lax.fori_loop(1, 8, hand_on, 0)
            own_copies[a].wait()

    def gather_wait(c, a):
        @pl.when(core != c)
        def _():
            def wait(d, carry):
                arrived(c, a, d)
                return carry
            lax.fori_loop(0, 8, wait, 0)

    gather_send(0)

    blocks = COLS // BLOCK
    for b in range(nk * blocks):
        lanes = slice((b % blocks) * BLOCK, (b % blocks + 1) * BLOCK)
        for pat, mask in ((pat_gate, mg), (pat_up, mu)):
            hit = jnp.where(pat[...] == hid * (nk * blocks) + b, 1.0, 0.0)
            hit = jnp.max(hit, axis=1, keepdims=True)
            mask[b // blocks, :, lanes] = jnp.broadcast_to(hit, (8, BLOCK))
    for b in range(8):
        hit = jnp.where(pat_down[...] == width * 8 + b, 1.0, 0.0)
        hit = jnp.max(hit, axis=1, keepdims=True)
        md[:, b * BLOCK:(b + 1) * BLOCK] = jnp.broadcast_to(hit, (nk * blocks, BLOCK))

    def split(s):
        return lax.div(s, nk), lax.rem(s, nk)

    def partials(s):
        half, k = split(s)
        slot = lax.rem(s, 3)

        @pl.when(s < nk)
        def _():
            for copy in weight_copies(k):
                copy.wait()
            for r in range(8):
                rows = slice(r * BLOCK, (r + 1) * BLOCK)
                for w, mask in ((wg, mg), (wu, mu)):
                    keep = jnp.broadcast_to(mask[k, r:r + 1, :], (BLOCK, COLS)).astype(BF16)
                    w[k, rows, :] = w[k, rows, :] * keep
            for i in range(blocks):
                rows = slice(i * BLOCK, (i + 1) * BLOCK)
                row = md[pl.ds(blocks * k + i, 1), :]
                keep = jnp.broadcast_to(row, (BLOCK, row.shape[1])).astype(BF16)
                wd[k, rows, :] = wd[k, rows, :] * keep

        for c in range(2):
            @pl.when(s == c * nk)
            def _():
                if c == 0:
                    gather_forward(c, 0)
                gather_wait(c, 0)

        def put(at, value):
            cols = slice(at * COLS, (at + 1) * COLS)
            own[slot, :, :, cols] = value[:192].reshape(4, 48, COLS)
            ysend[s, :, :, cols] = value[192:].astype(BF16).reshape(4, 48, COLS)

        x = tok[half].reshape(384, -1)
        put(0, jnp.dot(x, wg[k], preferred_element_type=F32))
        put(1, jnp.dot(x, wu[k], preferred_element_type=F32))
        for c in range(2):
            @pl.when(s == c * nk)
            def _():
                if c == 0:
                    gather_forward(c, 1)
                gather_wait(c, 1)
        put(2, nt(grd[half].reshape(384, -1), wd[k]))
        remote(ysend.at[s], yrecv.at[s], ys_sem.at[s], yr_sem.at[s], partner).start()

        @pl.when(s == 0)
        def _():
            gather_send(1)

        @pl.when(s == nk - 2)
        def _():
            gather_forward(1, 0)
            gather_forward(1, 1)

    def pair_sum(s, at):
        return own[lax.rem(s, 3), at] + yrecv[s, at].astype(F32)

    def after_pair(s):
        remote(ysend.at[s], yrecv.at[s], ys_sem.at[s], yr_sem.at[s], partner).wait_recv()
        for i, to in enumerate((zp, zm, zq)):
            zsend[s, i] = pair_sum(s, to).astype(BF16)
            remote(zsend.at[s, i], zrecv.at[s, i], zs_sem.at[s, i], zr_sem.at[s, i], at_z(to)).start()

    def ag_copy(s, i):
        src, to = (
            ((0, z), at_z(zp)), ((0, z), at_z(zm)), ((0, z), partner),
            ((1, z), at_z(zp)), ((1, z), at_z(zm)),
            ((0, zp), at_z(zm)), ((1, zm), at_z(zp)),
        )[i]
        here = ag.at[s, src[0], src[1]]
        there = ag.at[s, 1, z] if i == 2 else here
        return remote(here, there, as_sem.at[s, i], ar_sem.at[s, i], to)

    def ag_wait(s, i):
        y, at = ((0, zm), (0, zp), (1, z), (1, zm), (1, zp), (0, zq), (1, zq))[i]
        here = ag.at[s, y, at]
        remote(here, here, as_sem.at[s, i], ar_sem.at[s, i], partner).wait_recv()

    def activate(s):
        for i in range(3):
            remote(zsend.at[s, i], zrecv.at[s, i], zs_sem.at[s, i], zr_sem.at[s, i], at_z(zp)).wait_recv()
        total = pair_sum(s, z)
        for i in range(3):
            total = total + zrecv[s, i].astype(F32)
        gate, up, gh = total[:, :COLS], total[:, COLS:2 * COLS], total[:, 2 * COLS:]
        sig = 1.0 / (1.0 + jnp.exp(-gate))
        silu = gate * sig
        ag[s, 0, z, :, :COLS] = (silu * up).astype(BF16)
        ag[s, 0, z, :, COLS:2 * COLS] = (gh * up * sig * (1.0 + gate * (1.0 - sig))).astype(BF16)
        ag[s, 0, z, :, 2 * COLS:] = (gh * silu).astype(BF16)
        for i in (2, 0, 1):
            ag_copy(s, i).start()

    def pass_partner(s):
        ag_wait(s, 2)
        ag_copy(s, 3).start()
        ag_copy(s, 4).start()

    def pass_on(s):
        ag_wait(s, 1)
        ag_copy(s, 5).start()
        ag_wait(s, 3)
        ag_copy(s, 6).start()

    def back(s):
        half, k = split(s)
        for i in (0, 4, 5, 6):
            ag_wait(s, i)
        pltpu.make_async_copy(ag.at[s], act_out.at[s], act_sem.at[s]).start()

        @pl.when(k == 0)
        def _():
            acc[half] = jnp.zeros(acc.shape[1:], F32)

        hidden = ag[s, :, :, :, :COLS].reshape(384, COLS)
        d_gate = ag[s, :, :, :, COLS:2 * COLS].reshape(384, COLS)
        d_up = ag[s, :, :, :, 2 * COLS:].reshape(384, COLS)
        for n in range(4):
            cols = slice(n * 256, (n + 1) * 256)
            acc[half, 0, :, cols] += jnp.dot(hidden, wd[k, :, cols], preferred_element_type=F32)
            acc[half, 1, :, cols] += nt(d_gate, wg[k, cols, :]) + nt(d_up, wu[k, cols, :])

    def rows48(p):
        return pl.ds(pl.multiple_of(p * 48, 48), 48)

    def tail_pair(half):
        def send(d, carry):
            p = place(lax.rem(chip + d, 8))
            csend[half, p] = acc[half, 1 - core, rows48(p), :].astype(BF16)
            remote(csend.at[half, p], crecv.at[half, p], cs_sem.at[half, d], cr_sem.at[half, d], sibling).start()
            return carry
        lax.fori_loop(0, 8, send, 0)

    def tail_send(half):
        def send(d, carry):
            p = place(lax.rem(chip + d, 8))
            remote(csend.at[half, p], crecv.at[half, p], cs_sem.at[half, d], cr_sem.at[half, d], sibling).wait_recv()
            total = acc[half, core, rows48(p), :] + crecv[half, p].astype(F32)

            @pl.when(d > 0)
            def _():
                tsend[half, p] = total.astype(BF16)
                remote(tsend.at[half, p], trecv.at[core, d], ts_sem.at[half, d], tr_sem.at[core, d],
                       at_chip(lax.rem(chip + d, 8), half)).start()

            @pl.when((d == 0) & (core == half))
            def _():
                first[core] = total

            @pl.when((d == 0) & (core != half))
            def _():
                tsend[half, p] = total.astype(BF16)
                remote(tsend.at[half, p], trecv.at[core, 0], ts_sem.at[half, 0], tr_sem.at[core, 0], sibling).start()
            return carry
        lax.fori_loop(0, 8, send, 0)

    def tail_sum(half):
        @pl.when(core == half)
        def _():
            def landed(a, d):
                remote(trecv.at[a, d], trecv.at[a, d], ts_sem.at[half, d], tr_sem.at[a, d], sibling).wait_recv()
            landed(1 - half, 0)
            first[1 - half] = trecv[1 - half, 0].astype(F32)
            for a, out in enumerate((output, grad_tokens)):
                total = first[a]
                for d in range(1, 8):
                    landed(a, d)
                    total = total + trecv[a, d].astype(F32)
                out[...] = total.astype(BF16)

    last = steps + 5

    def step(t, carry):
        def run(offset, what):
            s = t - offset

            @pl.when((s >= 0) & (s < steps))
            def _():
                what(s)

        run(0, partials)
        run(1, after_pair)
        run(2, activate)
        run(3, pass_partner)
        run(4, pass_on)
        run(5, back)

        @pl.when(t == nk + 5)
        def _():
            tail_pair(0)
            pltpu.make_async_copy(tok, tok_out, all_sem.at[0]).start()
            pltpu.make_async_copy(grd, grd_out, all_sem.at[1]).start()

        @pl.when(t == nk + 6)
        def _():
            tail_send(0)
        return carry

    lax.fori_loop(0, last, step, 0)
    tail_pair(1)
    tail_send(1)
    tail_sum(0)
    tail_sum(1)

    def drain(s, carry):
        remote(ysend.at[s], yrecv.at[s], ys_sem.at[s], yr_sem.at[s], partner).wait_send()
        for i in range(3):
            remote(zsend.at[s, i], zrecv.at[s, i], zs_sem.at[s, i], zr_sem.at[s, i], partner).wait_send()
        for i in range(7):
            ag_copy(s, i).wait_send()
        pltpu.make_async_copy(ag.at[s], act_out.at[s], act_sem.at[s]).wait()
        return carry

    lax.fori_loop(0, steps, drain, 0)
    for a, (src, dst) in enumerate(pair):
        remote(src, dst.at[core, mine], hs_sem.at[a, 0], hr_sem.at[0, a, 0], sibling).wait_send()

        def gone(d, carry):
            remote(src, dst.at[core, mine], hs_sem.at[a, d], hr_sem.at[0, a, d], sibling).wait_send()
            there = dst.at[core, place(lax.rem(chip + 8 - d, 8))]
            remote(there, there, hf_sem.at[a, d], hr_sem.at[0, a, d], sibling).wait_send()
            return carry
        lax.fori_loop(1, 8, gone, 0)
    for half in range(2):
        def sent(d, carry):
            p = place(lax.rem(chip + d, 8))
            remote(csend.at[half, p], crecv.at[half, p], cs_sem.at[half, d], cr_sem.at[half, d], sibling).wait_send()

            @pl.when((d > 0) | (core != half))
            def _():
                remote(tsend.at[half, p], trecv.at[core, d], ts_sem.at[half, d], tr_sem.at[core, d], sibling).wait_send()
            return carry
        lax.fori_loop(0, 8, sent, 0)
    pltpu.make_async_copy(tok, tok_out, all_sem.at[0]).wait()
    pltpu.make_async_copy(grd, grd_out, all_sem.at[1]).wait()


def layer(tokens, gate_w, up_w, down_w, grad_out, pat_gate, pat_up, pat_down):
    rows, width = tokens.shape
    hidden = gate_w.shape[1]
    nk = hidden // COLS
    steps = 2 * nk
    any_, vmem = pl.BlockSpec(memory_space=pl.ANY), pl.BlockSpec(memory_space=pltpu.VMEM)
    dma, three = pltpu.SemaphoreType.DMA, 3 * COLS
    small = jax.ShapeDtypeStruct((rows, width), BF16)
    gathered = jax.ShapeDtypeStruct((2, 8, rows, width), BF16)
    return pl.pallas_call(
        functools.partial(layer_kernel, nk),
        name="layer",
        out_shape=(small, small, jax.ShapeDtypeStruct((steps, 2, 4, rows, three), BF16), gathered, gathered),
        in_specs=[any_] * 5 + [vmem] * 3,
        out_specs=(vmem, vmem, any_, any_, any_),
        scratch_shapes=[
            pltpu.VMEM((nk, width, COLS), BF16),
            pltpu.VMEM((nk, width, COLS), BF16),
            pltpu.VMEM((nk, COLS, width), BF16),
            pltpu.VMEM((nk, 8, COLS), F32),
            pltpu.VMEM((nk, 8, COLS), F32),
            pltpu.VMEM((hidden // BLOCK, width), F32),
            pltpu.VMEM((2, 8, rows, width), BF16),
            pltpu.VMEM((2, 8, rows, width), BF16),
            pltpu.VMEM((3, 4, rows, three), F32),
            pltpu.VMEM((steps, 4, rows, three), BF16),
            pltpu.VMEM((steps, 4, rows, three), BF16),
            pltpu.VMEM((steps, 3, rows, three), BF16),
            pltpu.VMEM((steps, 3, rows, three), BF16),
            pltpu.VMEM((steps, 2, 4, rows, three), BF16),
            pltpu.VMEM((2, 2, 8 * rows, width), F32),
            pltpu.VMEM((2, 8, rows, width), BF16),
            pltpu.VMEM((2, 8, rows, width), BF16),
            pltpu.VMEM((2, 8, rows, width), BF16),
            pltpu.VMEM((2, 8, rows, width), BF16),
            pltpu.VMEM((2, rows, width), F32),
            dma((3, nk)), dma((2,)), dma((2, 8)), dma((2, 2, 8)), dma((2, 8)),
            dma((steps,)), dma((steps,)), dma((steps, 3)), dma((steps, 3)),
            dma((steps, 7)), dma((steps, 7)), dma((2, 8)), dma((2, 8)),
            dma((2, 8)), dma((2, 8)), dma((steps,)), dma((2,)),
        ],
        compiler_params=pltpu.CompilerParams(
            collective_id=0, has_side_effects=True, vmem_limit_bytes=60 * 2**20
        ),
    )(tokens, gate_w, up_w, down_w, grad_out, pat_gate, pat_up, pat_down)


def weight_grads_kernel(act, tok, grd, pat_gate, pat_up, pat_down, grad_gate, grad_up, grad_down):
    k = pl.program_id(0)
    hid = lax.axis_index("hidden")
    width = lax.axis_index("width")
    blocks = COLS // BLOCK
    per = pl.num_programs(0) * blocks
    contract = (((0,), (0,)), ((), ()))
    rows = tok.shape[0]
    x = tok[...]
    for at, pat, out in ((1, pat_gate, grad_gate), (2, pat_up, grad_up)):
        d = act[:, 0, :, at * COLS:(at + 1) * COLS].reshape(rows, COLS)
        res = lax.dot_general(x, d, contract, preferred_element_type=F32)
        for b in range(blocks):
            hit = jnp.where(pat[...] == hid * per + k * blocks + b, 1.0, 0.0)
            hit = jnp.max(hit, axis=1, keepdims=True)
            lanes = slice(b * BLOCK, (b + 1) * BLOCK)
            for r in range(8):
                rs = slice(r * BLOCK, (r + 1) * BLOCK)
                keep = jnp.broadcast_to(hit[r:r + 1, :], (BLOCK, BLOCK))
                out[rs, lanes] = jnp.where(keep > 0.0, res[rs, lanes], 0.0).astype(BF16)
    h = act[:, 0, :, :COLS].reshape(rows, COLS)
    res = lax.dot_general(h, grd[...], contract, preferred_element_type=F32)
    for i in range(blocks):
        row = pat_down[pl.ds(k * blocks + i, 1), :]
        rs = slice(i * BLOCK, (i + 1) * BLOCK)
        for b in range(8):
            hit = jnp.max(jnp.where(row == width * 8 + b, 1.0, 0.0), axis=1, keepdims=True)
            lanes = slice(b * BLOCK, (b + 1) * BLOCK)
            keep = jnp.broadcast_to(hit, (BLOCK, BLOCK))
            grad_down[rs, lanes] = jnp.where(keep > 0.0, res[rs, lanes], 0.0).astype(BF16)


def weight_grads(act, tok, grd, pat_gate, pat_up, pat_down):
    nk = act.shape[0] // 2
    tokens, width = 2 * act.shape[1], tok.shape[1]
    hidden = nk * COLS
    whole = lambda k: (0, 0)
    return pl.pallas_call(
        weight_grads_kernel,
        name="weight_grads",
        grid=(nk,),
        out_shape=(
            jax.ShapeDtypeStruct((width, hidden), BF16),
            jax.ShapeDtypeStruct((width, hidden), BF16),
            jax.ShapeDtypeStruct((hidden, width), BF16),
        ),
        in_specs=[
            pl.BlockSpec((2, 1, tokens // 2, 3 * COLS), lambda k: (0, k, 0, 0)),
            pl.BlockSpec((tokens, width), whole),
            pl.BlockSpec((tokens, width), whole),
            pl.BlockSpec(pat_gate.shape, whole),
            pl.BlockSpec(pat_up.shape, whole),
            pl.BlockSpec(pat_down.shape, whole),
        ],
        out_specs=(
            pl.BlockSpec((width, COLS), lambda k: (0, k)),
            pl.BlockSpec((width, COLS), lambda k: (0, k)),
            pl.BlockSpec((COLS, width), lambda k: (k, 0)),
        ),
        compiler_params=pltpu.CompilerParams(vmem_limit_bytes=48 * 2**20),
    )(act.reshape(2, nk, tokens // 2, 3 * COLS), tok, grd, pat_gate, pat_up, pat_down)


def per_device(
    tokens, gate_weight, up_weight, down_weight, grad_out, pattern_gate, pattern_up, pattern_down
):
    output, grad_tokens, act, tok, grd = layer(
        tokens, gate_weight, up_weight, down_weight, grad_out, pattern_gate, pattern_up, pattern_down
    )
    rows, width = tokens.shape
    grad_gate, grad_up, grad_down = weight_grads(
        act.reshape(act.shape[0], 8 * rows, 3 * COLS),
        tok.reshape(16 * rows, width),
        grd.reshape(16 * rows, width),
        pattern_gate, pattern_up, pattern_down,
    )
    return output, grad_tokens, grad_gate, grad_up, grad_down


def solution(mesh):
    placed = (
        P("hidden", "width"),
        P("width", "hidden"),
        P("width", "hidden"),
        P("hidden", "width"),
        P("hidden", "width"),
        P("width", None),
        P("width", None),
        P("hidden", None),
    )
    return jax.shard_map(
        per_device,
        mesh=mesh,
        in_specs=placed,
        out_specs=(
            P("hidden", "width"),
            P("hidden", "width"),
            P("width", "hidden"),
            P("width", "hidden"),
            P("hidden", "width"),
        ),
        check_vma=False,
    )
```

```python
import functools

import jax
import jax.numpy as jnp
from jax import lax
from jax.experimental import pallas as pl
from jax.experimental.pallas import tpu as pltpu
from jax.sharding import PartitionSpec as P

BLOCK = 128
COLS = 256
PARTS = 3
PIECE = 16
LAGS = (0, 1, 2, 3, 4, 5)
SLOTS = 4
DIRECT = 1
CUTS = 8
MESH = pl.DeviceIdType.MESH
F32 = jnp.float32
BF16 = jnp.bfloat16


def remote(src, dst, send, recv, device):
    return pltpu.make_async_remote_copy(
        src_ref=src, dst_ref=dst, send_sem=send, recv_sem=recv,
        device_id=device, device_id_type=MESH,
    )


def nt(a, b):
    return lax.dot_general(a, b, (((1,), (1,)), ((), ())), preferred_element_type=F32)


def layer_kernel(
    nk,
    tokens, gate_w, up_w, down_w, grad_out, pat_gate, pat_up, pat_down,
    output, grad_tokens, grad_gate, grad_up, grad_down,
    wg, wu, wd, mg, mu, md, tok, grd, own, ysend, yrecv, zsend, zrecv, ag, acc,
    crecv, xsend, xrecv, kept, fsend, frecv, gg, gu, gd, lsend, lrecv,
    w_sem, o_sem, hs_sem, hr_sem, ys_sem, yr_sem, zs_sem, zr_sem,
    as_sem, ar_sem, cs_sem, cr_sem, xs_sem, xr_sem, fs_sem, fr_sem, g_sem, ls_sem, lr_sem, y0_sem,
):
    steps = PARTS * nk
    width = lax.axis_index("width")
    hid = lax.axis_index("hidden")
    z = lax.rem(width, 4)
    yl = lax.div(width, 4)
    core = lax.rem(hid, 2)
    yh = lax.rem(lax.div(hid, 2), 2)
    x = lax.div(hid, 4)
    zp, zm, zq = lax.rem(z + 1, 4), lax.rem(z + 3, 4), lax.rem(z + 2, 4)
    xp, xm, xq = lax.rem(x + 1, 4), lax.rem(x + 3, 4), lax.rem(x + 2, 4)

    def at_z(to):
        return (yl * 4 + to, hid)

    def other_y(to):
        return ((1 - yl) * 4 + to, hid)

    def at_chip(its_x, its_yh):
        return (width, its_x * 4 + its_yh * 2 + core)

    def at_x(to):
        return at_chip(to, yh)

    partner = ((1 - yl) * 4 + z, hid)
    sibling = (width, hid + 1 - 2 * core)
    across = (width, x * 4 + (1 - yh) * 2 + core)

    def place(its_x, its_yh):
        return lax.rem(its_x * 2 + its_yh + 4 * yl, 8)

    def weight_copies(k):
        cols = pl.ds(k * COLS, COLS) if isinstance(k, int) else pl.ds(pl.multiple_of(k * COLS, COLS), COLS)
        return (
            pltpu.make_async_copy(gate_w.at[:, cols], wg.at[k], w_sem.at[0, k]),
            pltpu.make_async_copy(up_w.at[:, cols], wu.at[k], w_sem.at[1, k]),
            pltpu.make_async_copy(down_w.at[cols, :], wd.at[k], w_sem.at[2, k]),
        )

    pair = ((tokens, tok), (grad_out, grd))

    def own_copy(p, a):
        src, dst = pair[a]
        return pltpu.make_async_copy(
            src.at[pl.ds(p * PIECE, PIECE)], dst.at[p, place(x, yh), core], o_sem.at[a, p]
        )

    for p in range(PARTS):
        for a in range(2):
            own_copy(p, a).start()
    for copy in weight_copies(0):
        copy.start()

    barrier = pltpu.get_barrier_semaphore()
    friends = [at_z(zp), at_z(zm), at_z(zq), partner, other_y(zp), other_y(zm), other_y(zq), sibling, across]
    friends += [at_chip(to, its_yh) for to in (xp, xm, xq) for its_yh in (yh, 1 - yh)]
    for friend in friends:
        pl.semaphore_signal(barrier, inc=1, device_id=friend, device_id_type=MESH)
    pl.semaphore_wait(barrier, len(friends))

    def gathered(p, a, i):
        its_x = (x, x, xm, xp, xq, xm, xp, xq)[i if i < 8 else i - 7]
        its_yh = (yh, 1 - yh, yh, yh, yh, 1 - yh, 1 - yh, 1 - yh)[i if i < 8 else i - 7]
        its_core = core if 0 < i < 8 else 1 - core
        return pair[a][1].at[p, place(its_x, its_yh), its_core]

    def gather_copy(p, a, i):
        to = (sibling, across, at_x(xp), at_x(xm), at_x(xq), at_x(xp), at_x(xm), at_x(xq))
        if i < 5:
            src = dst = pair[a][1].at[p, place(x, yh), core]
        elif i < 8 and p == 0:
            src = dst = pair[a][1].at[p, place(x, yh), core]
        elif i < 8:
            src = dst = gathered(p, a, 1)
        else:
            src = dst = gathered(p, a, i - 7)
        if p == 0:
            to = to[:5] + (at_chip(xp, 1 - yh), at_chip(xm, 1 - yh), at_chip(xq, 1 - yh))
        return remote(src, dst, hs_sem.at[p, a, i], hr_sem.at[p, a, i], to[i] if i < 8 else sibling)

    def gather_arrived(p, a, i):
        dst = gathered(p, a, i)
        remote(dst, dst, hs_sem.at[p, a, i], hr_sem.at[p, a, i], sibling).wait_recv()

    def gather_send(p, a):
        own_copy(p, a).wait()
        for i in (1, 5, 6, 7, 2, 3, 4, 0) if p == 0 else (1, 2, 3, 4, 0):
            gather_copy(p, a, i).start()

    def gather_across(p, a):
        gather_arrived(p, a, 1)
        for i in (8,) if p == 0 else (5, 6, 7, 8):
            gather_copy(p, a, i).start()

    def gather_share(p, a):
        for i in range(2, 8):
            gather_arrived(p, a, i)
            gather_copy(p, a, i + 7).start()

    def gather_wait(p, a):
        for i in (0, *range(8, 15)):
            gather_arrived(p, a, i)

    for a in range(2):
        gather_send(0, a)
    for k in range(1, nk):
        for copy in weight_copies(k):
            copy.start()

    blocks = COLS // BLOCK
    for b in range(nk * blocks):
        lanes = slice((b % blocks) * BLOCK, (b % blocks + 1) * BLOCK)
        for pat, mask in ((pat_gate, mg), (pat_up, mu)):
            hit = jnp.where(pat[...] == hid * (nk * blocks) + b, 1.0, 0.0)
            hit = jnp.max(hit, axis=1, keepdims=True)
            mask[b // blocks, :, lanes] = jnp.broadcast_to(hit, (8, BLOCK))
    for b in range(8):
        hit = jnp.where(pat_down[...] == width * 8 + b, 1.0, 0.0)
        hit = jnp.max(hit, axis=1, keepdims=True)
        md[:, b * BLOCK:(b + 1) * BLOCK] = jnp.broadcast_to(hit, (nk * blocks, BLOCK))

    def split(s):
        return lax.div(s, nk), lax.rem(s, nk)

    rows = 16 * PIECE
    half, slot_rows = rows // 2, rows // 8

    def masked_weights(k):
        for copy in weight_copies(k):
            copy.wait()
        for r in range(8):
            at = slice(r * BLOCK, (r + 1) * BLOCK)
            for w, mask in ((wg, mg), (wu, mu)):
                keep = jnp.broadcast_to(mask[k, r:r + 1, :], (BLOCK, COLS)).astype(BF16)
                w[k, at, :] = w[k, at, :] * keep
        for i in range(blocks):
            at = slice(i * BLOCK, (i + 1) * BLOCK)
            row = md[pl.ds(blocks * k + i, 1), :]
            keep = jnp.broadcast_to(row, (BLOCK, row.shape[1])).astype(BF16)
            wd[k, at, :] = wd[k, at, :] * keep

    def first_copy(i):
        cols = (pl.ds(0, 2 * COLS), pl.ds(2 * COLS, COLS))[i]
        return remote(ysend.at[0, :, :, cols], yrecv.at[0, :, :, cols], y0_sem.at[i], y0_sem.at[2 + i], partner)

    def partials(s):
        part, k = split(s)
        slot = lax.rem(s, SLOTS)

        @pl.when(s < nk)
        def _():
            masked_weights(k)

        for p in range(1, PARTS):
            @pl.when(s == p * nk)
            def _():
                gather_wait(p, 0)
                gather_wait(p, 1)

        @pl.when(s == 0)
        def _():
            gather_across(0, 0)
            gather_share(0, 0)
            gather_wait(0, 0)

        def put(at, value):
            cols = slice(at * COLS, (at + 1) * COLS)
            own[slot, :, :, cols] = value[:half].reshape(4, slot_rows, COLS)
            ysend[s, :, :, cols] = value[half:].astype(BF16).reshape(4, slot_rows, COLS)

        t = tok[part].reshape(rows, -1)
        put(0, jnp.dot(t, wg[k], preferred_element_type=F32))
        put(1, jnp.dot(t, wu[k], preferred_element_type=F32))

        @pl.when(s == 0)
        def _():
            first_copy(0).start()
            gather_across(0, 1)
            gather_share(0, 1)
            gather_wait(0, 1)
        put(2, nt(grd[part].reshape(rows, -1), wd[k]))

        @pl.when(s == 0)
        def _():
            first_copy(1).start()

        @pl.when(s > 0)
        def _():
            remote(ysend.at[s], yrecv.at[s], ys_sem.at[s], yr_sem.at[s], partner).start()

        for p in range(1, PARTS):
            for at, what in ((0, gather_send), (2, gather_across), (4, gather_share)):
                @pl.when(s == (p - 1) * nk + at)
                def _():
                    what(p, 0)
                    what(p, 1)

    def pair_sum(s, at):
        return own[lax.rem(s, SLOTS), at] + yrecv[s, at].astype(F32)

    def after_pair(s):
        @pl.when(s == 0)
        def _():
            for i in range(2):
                first_copy(i).wait_recv()

        @pl.when(s > 0)
        def _():
            remote(ysend.at[s], yrecv.at[s], ys_sem.at[s], yr_sem.at[s], partner).wait_recv()
        for i, to in enumerate((zp, zm, zq)):
            zsend[s, i] = pair_sum(s, to).astype(BF16)
            remote(zsend.at[s, i], zrecv.at[s, i], zs_sem.at[s, i], zr_sem.at[s, i], at_z(to)).start()

    def ag_copy(s, i):
        src, to = (
            ((0, z), at_z(zp)), ((0, z), at_z(zm)), ((0, z), partner),
            ((1, z), at_z(zp)), ((1, z), at_z(zm)),
            ((0, zp), at_z(zm)), ((1, zm), at_z(zp)),
        )[i]
        here = ag.at[s, src[0], src[1]]
        there = ag.at[s, 1, z] if i == 2 else here
        return remote(here, there, as_sem.at[s, i], ar_sem.at[s, i], to)

    def ag_direct(s, i):
        to = (other_y(zp), other_y(zm), at_z(zq), other_y(zq))[i - 3]
        there = ag.at[s, 0 if i == 5 else 1, z]
        return remote(ag.at[s, 0, z], there, as_sem.at[s, i], ar_sem.at[s, i], to)

    def ag_wait(s, i):
        y, at = ((0, zm), (0, zp), (1, z), (1, zm), (1, zp), (0, zq), (1, zq))[i]
        here = ag.at[s, y, at]
        remote(here, here, as_sem.at[s, i], ar_sem.at[s, i], partner).wait_recv()

    def activate(s):
        for i in range(3):
            remote(zsend.at[s, i], zrecv.at[s, i], zs_sem.at[s, i], zr_sem.at[s, i], at_z(zp)).wait_recv()
        total = pair_sum(s, z)
        for i in range(3):
            total = total + zrecv[s, i].astype(F32)
        gate, up, gh = total[:, :COLS], total[:, COLS:2 * COLS], total[:, 2 * COLS:]
        sig = 1.0 / (1.0 + jnp.exp(-gate))
        silu = gate * sig
        ag[s, 0, z, :, :COLS] = (silu * up).astype(BF16)
        ag[s, 0, z, :, COLS:2 * COLS] = (gh * up * sig * (1.0 + gate * (1.0 - sig))).astype(BF16)
        ag[s, 0, z, :, 2 * COLS:] = (gh * silu).astype(BF16)
        for i in (2, 0, 1):
            ag_copy(s, i).start()

        @pl.when(s >= steps - DIRECT)
        def _():
            for i in (3, 4, 5, 6):
                ag_direct(s, i).start()

    def pass_partner(s):
        ag_wait(s, 2)

        @pl.when(s < steps - DIRECT)
        def _():
            ag_copy(s, 3).start()
            ag_copy(s, 4).start()

    def pass_on(s):
        ag_wait(s, 1)

        @pl.when(s < steps - DIRECT)
        def _():
            ag_copy(s, 5).start()
        ag_wait(s, 3)

        @pl.when(s < steps - DIRECT)
        def _():
            ag_copy(s, 6).start()

    def back(s):
        part, k = split(s)
        slot = lax.rem(part, 2)
        for i in (0, 4, 5, 6):
            ag_wait(s, i)

        @pl.when(s == 2 * nk)
        def _():
            for i in range(8):
                tail_copy(0, i).wait_send()

        @pl.when(k == 0)
        def _():
            acc[slot] = jnp.zeros(acc.shape[1:], F32)

        hidden = ag[s, :, :, :, :COLS].reshape(rows, COLS)
        d_gate = ag[s, :, :, :, COLS:2 * COLS].reshape(rows, COLS)
        d_up = ag[s, :, :, :, 2 * COLS:].reshape(rows, COLS)
        for n in range(4):
            cols = slice(n * 256, (n + 1) * 256)
            acc[slot, 0, :, cols] += jnp.dot(hidden, wd[k, :, cols], preferred_element_type=F32)
            acc[slot, 1, :, cols] += nt(d_gate, wg[k, cols, :]) + nt(d_up, wu[k, cols, :])

    def tail_chip(i):
        return (xp, xm, xq, x)[i // 2], i % 2

    def tail_rows(i, its_core):
        return pl.ds(pl.multiple_of(place(*tail_chip(i)) * slot_rows + its_core * PIECE, PIECE), PIECE)

    def tail_copy(p, i):
        return remote(
            acc.at[p % 2, :, tail_rows(i, 1 - core), :], crecv.at[p, i], cs_sem.at[p, i], cr_sem.at[p, i], sibling
        )

    def tail_pair(p):
        for i in range(8):
            tail_copy(p, i).start()

    def core_sum(p, i):
        return acc[p % 2, :, tail_rows(i, core), :] + crecv[p, i]

    def x_copy(p, i):
        return remote(xsend.at[p, i], xrecv.at[p, i], xs_sem.at[p, i], xr_sem.at[p, i], at_x((xp, xm, xq)[i]))

    def tail_x(p):
        for i in range(8):
            tail_copy(p, i).wait_recv()
            if i < 6:
                xsend[p, i // 2, i % 2] = core_sum(p, i).astype(BF16)
                if i % 2 == 1:
                    x_copy(p, i // 2).start()

    def across_copy(p):
        return remote(fsend.at[p], frecv.at[p], fs_sem.at[p], fr_sem.at[p], across)

    def tail_y(p):
        for i in range(3):
            x_copy(p, i).wait_recv()
        for its_yh in range(2):
            total = core_sum(p, 6 + its_yh)
            for i in range(3):
                total = total + xrecv[p, i, its_yh].astype(F32)

            @pl.when(yh == its_yh)
            def _():
                kept[p] = total

            @pl.when(yh != its_yh)
            def _():
                fsend[p] = total.astype(BF16)
        across_copy(p).start()

    def tail_end(p):
        across_copy(p).wait_recv()
        at = slice(p * PIECE, (p + 1) * PIECE)
        output[at, :] = (kept[p, 0] + frecv[p, 0].astype(F32)).astype(BF16)
        grad_tokens[at, :] = (kept[p, 1] + frecv[p, 1].astype(F32)).astype(BF16)

    def last_copy(i):
        its_x, its_yh = ((xp, yh), (xm, yh), (xp, 1 - yh), (xm, 1 - yh), (xq, yh), (xq, 1 - yh), (x, 1 - yh))[i]
        return remote(lsend.at[i], lrecv.at[i], ls_sem.at[i], lr_sem.at[i], at_chip(its_x, its_yh))

    def last_slot(i):
        return ((0, yh), (1, yh), (0, 1 - yh), (1, 1 - yh), (2, yh), (2, 1 - yh), (3, 1 - yh), (3, yh))[i]

    def last_sum_of(i):
        its_x, its_yh = last_slot(i)
        place_x = (xp, xm, xq, x)[its_x]
        at = pl.ds(pl.multiple_of(place(place_x, its_yh) * slot_rows + core * PIECE, PIECE), PIECE)
        return acc[(PARTS - 1) % 2, :, at, :] + crecv[PARTS - 1, its_x * 2 + its_yh]

    def last_send():
        for i in range(8):
            tail_copy(PARTS - 1, i).wait_recv()
            if i % 2 == 1:
                for j in ((0, 2), (1, 3), (4, 5), (6,))[i // 2]:
                    lsend[j] = last_sum_of(j).astype(BF16)
                    last_copy(j).start()

    def last_sum():
        total = last_sum_of(7)
        for i in range(7):
            last_copy(i).wait_recv()
            total = total + lrecv[i].astype(F32)
        at = slice((PARTS - 1) * PIECE, PARTS * PIECE)
        output[at, :] = total[0].astype(BF16)
        grad_tokens[at, :] = total[1].astype(BF16)

    def grad_copies(k):
        cols = pl.ds(k * COLS, COLS) if isinstance(k, int) else pl.ds(pl.multiple_of(k * COLS, COLS), COLS)
        at = k % 2 if isinstance(k, int) else lax.rem(k, 2)
        return (
            pltpu.make_async_copy(gg.at[at], grad_gate.at[:, cols], g_sem.at[at, 0]),
            pltpu.make_async_copy(gu.at[at], grad_up.at[:, cols], g_sem.at[at, 1]),
            pltpu.make_async_copy(gd.at[at], grad_down.at[cols, :], g_sem.at[at, 2]),
        )

    def weight_grads(k):
        at = k % 2 if isinstance(k, int) else lax.rem(k, 2)

        @pl.when(k >= 2)
        def _():
            for copy in grad_copies(k - 2):
                copy.wait()

        def units(i):
            cols = slice(i * COLS, (i + 1) * COLS)
            return jnp.concatenate(
                [ag[p * nk + k, :, :, :, cols].reshape(rows, COLS) for p in range(PARTS)], axis=0
            )

        contract = (((0,), (0,)), ((), ()))
        hidden, d_gate, d_up = units(0), units(1), units(2)
        for n in range(4):
            cols = slice(n * 256, (n + 1) * 256)
            t = tok[:, :, :, :, cols].reshape(PARTS * rows, 256)
            for d, mask, out in ((d_gate, mg, gg), (d_up, mu, gu)):
                res = lax.dot_general(t, d, contract, preferred_element_type=F32)
                for r in range(2):
                    keep = jnp.broadcast_to(mask[k, 2 * n + r:2 * n + r + 1, :], (BLOCK, COLS))
                    kept_rows = jnp.where(keep > 0.0, res[r * BLOCK:(r + 1) * BLOCK], 0.0)
                    out[at, (2 * n + r) * BLOCK:(2 * n + r + 1) * BLOCK, :] = kept_rows.astype(BF16)
            g = grd[:, :, :, :, cols].reshape(PARTS * rows, 256)
            res = lax.dot_general(hidden, g, contract, preferred_element_type=F32)
            for i in range(blocks):
                row = md[pl.ds(blocks * k + i, 1), cols]
                keep = jnp.broadcast_to(row, (BLOCK, 256))
                kept_rows = jnp.where(keep > 0.0, res[i * BLOCK:(i + 1) * BLOCK], 0.0)
                gd[at, i * BLOCK:(i + 1) * BLOCK, cols] = kept_rows.astype(BF16)
        for copy in grad_copies(k):
            copy.start()

    lag = LAGS[-1]

    def step(t, carry):
        def run(offset, what):
            s = t - offset

            @pl.when((s >= 0) & (s < steps))
            def _():
                what(s)

        k = t - LAGS[-1] - 1 - (PARTS - 1) * nk

        @pl.when(k >= 0)
        def _():
            weight_grads(k)

        for offset, what in zip(LAGS, (partials, after_pair, activate, pass_partner, pass_on, back)):
            run(offset, what)

        for p in range(PARTS - 1):
            for after, what in enumerate((tail_pair, tail_x, tail_y, tail_end)):
                @pl.when(t == (p + 1) * nk - 1 + lag + after)
                def _():
                    what(p)
        return carry

    lax.fori_loop(0, steps + lag, step, 0)
    tail_pair(PARTS - 1)
    last_send()
    weight_grads(nk - 1)
    last_sum()

    def drain(s, carry):
        @pl.when(s > 0)
        def _():
            remote(ysend.at[s], yrecv.at[s], ys_sem.at[s], yr_sem.at[s], partner).wait_send()
        for i in range(3):
            remote(zsend.at[s, i], zrecv.at[s, i], zs_sem.at[s, i], zr_sem.at[s, i], partner).wait_send()
        for i in range(7):
            ag_copy(s, i).wait_send()
        return carry

    lax.fori_loop(0, steps, drain, 0)
    for i in range(2):
        first_copy(i).wait_send()
    for p in range(PARTS):
        for a in range(2):
            for i in range(15):
                gather_copy(p, a, i).wait_send()
        if p > 0:
            for i in range(8):
                tail_copy(p, i).wait_send()
        if p < PARTS - 1:
            for i in range(3):
                x_copy(p, i).wait_send()
            across_copy(p).wait_send()
    for i in range(7):
        last_copy(i).wait_send()
    for k in (nk - 2, nk - 1):
        for copy in grad_copies(k):
            copy.wait()


def layer(tokens, gate_w, up_w, down_w, grad_out, pat_gate, pat_up, pat_down):
    rows, width = tokens.shape
    hidden = gate_w.shape[1]
    nk = hidden // COLS
    steps = PARTS * nk
    any_, vmem = pl.BlockSpec(memory_space=pl.ANY), pl.BlockSpec(memory_space=pltpu.VMEM)
    dma, three, slot_rows = pltpu.SemaphoreType.DMA, 3 * COLS, 2 * PIECE
    small = jax.ShapeDtypeStruct((rows, width), BF16)
    whole = (PARTS, 8, 2, PIECE, width)
    return pl.pallas_call(
        functools.partial(layer_kernel, nk),
        name="layer",
        out_shape=(
            small, small,
            jax.ShapeDtypeStruct((width, hidden), BF16),
            jax.ShapeDtypeStruct((width, hidden), BF16),
            jax.ShapeDtypeStruct((hidden, width), BF16),
        ),
        in_specs=[any_] * 5 + [vmem] * 3,
        out_specs=(vmem, vmem, any_, any_, any_),
        scratch_shapes=[
            pltpu.VMEM((nk, width, COLS), BF16),
            pltpu.VMEM((nk, width, COLS), BF16),
            pltpu.VMEM((nk, COLS, width), BF16),
            pltpu.VMEM((nk, 8, COLS), F32),
            pltpu.VMEM((nk, 8, COLS), F32),
            pltpu.VMEM((hidden // BLOCK, width), F32),
            pltpu.VMEM(whole, BF16),
            pltpu.VMEM(whole, BF16),
            pltpu.VMEM((SLOTS, 4, slot_rows, three), F32),
            pltpu.VMEM((steps, 4, slot_rows, three), BF16),
            pltpu.VMEM((steps, 4, slot_rows, three), BF16),
            pltpu.VMEM((steps, 3, slot_rows, three), BF16),
            pltpu.VMEM((steps, 3, slot_rows, three), BF16),
            pltpu.VMEM((steps, 2, 4, slot_rows, three), BF16),
            pltpu.VMEM((2, 2, 16 * PIECE, width), F32),
            pltpu.VMEM((PARTS, 8, 2, PIECE, width), F32),
            pltpu.VMEM((PARTS, 3, 2, 2, PIECE, width), BF16),
            pltpu.VMEM((PARTS, 3, 2, 2, PIECE, width), BF16),
            pltpu.VMEM((PARTS, 2, PIECE, width), F32),
            pltpu.VMEM((PARTS, 2, PIECE, width), BF16),
            pltpu.VMEM((PARTS, 2, PIECE, width), BF16),
            pltpu.VMEM((2, width, COLS), BF16),
            pltpu.VMEM((2, width, COLS), BF16),
            pltpu.VMEM((2, COLS, width), BF16),
            pltpu.VMEM((7, 2, PIECE, width), BF16),
            pltpu.VMEM((7, 2, PIECE, width), BF16),
            dma((3, nk)), dma((2, PARTS)), dma((PARTS, 2, 15)), dma((PARTS, 2, 15)),
            dma((steps,)), dma((steps,)), dma((steps, 3)), dma((steps, 3)),
            dma((steps, 7)), dma((steps, 7)), dma((PARTS, 8)), dma((PARTS, 8)),
            dma((PARTS, 3)), dma((PARTS, 3)), dma((PARTS,)), dma((PARTS,)),
            dma((2, 3)), dma((7,)), dma((7,)), dma((4,)),
        ],
        compiler_params=pltpu.CompilerParams(
            collective_id=0, has_side_effects=True, vmem_limit_bytes=60 * 2**20
        ),
    )(tokens, gate_w, up_w, down_w, grad_out, pat_gate, pat_up, pat_down)


def hand_out_kernel(*refs):
    n = len(refs) // 2
    for src, dst in zip(refs[:n], refs[n:]):
        dst[...] = src[...]


def hand_out(*arrays):
    specs = tuple(pl.BlockSpec((a.shape[0] // CUTS, a.shape[1]), lambda i: (i, 0)) for a in arrays)
    return pl.pallas_call(
        hand_out_kernel,
        name="hand_out",
        grid=(CUTS,),
        out_shape=tuple(jax.ShapeDtypeStruct(a.shape, a.dtype) for a in arrays),
        in_specs=list(specs),
        out_specs=specs,
        compiler_params=pltpu.CompilerParams(vmem_limit_bytes=60 * 2**20),
    )(*arrays)


def per_device(*args):
    output, grad_tokens, *grads = layer(*args)
    return output, grad_tokens, *hand_out(*grads)


def solution(mesh):
    placed = (
        P("hidden", "width"),
        P("width", "hidden"),
        P("width", "hidden"),
        P("hidden", "width"),
        P("hidden", "width"),
        P("width", None),
        P("width", None),
        P("hidden", None),
    )
    return jax.shard_map(
        per_device,
        mesh=mesh,
        in_specs=placed,
        out_specs=(
            P("hidden", "width"),
            P("hidden", "width"),
            P("width", "hidden"),
            P("width", "hidden"),
            P("hidden", "width"),
        ),
        check_vma=False,
    )
```

```python
import functools

import jax
import jax.numpy as jnp
from jax import lax
from jax.experimental import pallas as pl
from jax.experimental.pallas import tpu as pltpu
from jax.sharding import PartitionSpec as P

BLOCK = 128
COLS = 256
PARTS = 3
PIECE = 16
LAGS = (0, 1, 2, 3, 4, 5)
SLOTS = 4
DIRECT = 1
CUTS = 4
MESH = pl.DeviceIdType.MESH
F32 = jnp.float32
BF16 = jnp.bfloat16


def remote(src, dst, send, recv, device):
    return pltpu.make_async_remote_copy(
        src_ref=src, dst_ref=dst, send_sem=send, recv_sem=recv,
        device_id=device, device_id_type=MESH,
    )


def nt(a, b):
    return lax.dot_general(a, b, (((1,), (1,)), ((), ())), preferred_element_type=F32)


def layer_kernel(
    nk,
    tokens, gate_w, up_w, down_w, grad_out, pat_gate, pat_up, pat_down,
    output, grad_tokens, grad_gate, grad_up, grad_down,
    wg, wu, wd, mg, mu, md, tok, grd, own, ysend, yrecv, zsend, zrecv, ag, acc,
    crecv, xsend, xrecv, kept, fsend, frecv, gg, gu, gd, lsend, lrecv,
    w_sem, o_sem, hs_sem, hr_sem, ys_sem, yr_sem, zs_sem, zr_sem,
    as_sem, ar_sem, cs_sem, cr_sem, xs_sem, xr_sem, fs_sem, fr_sem, g_sem, ls_sem, lr_sem, y0_sem, yd_sem,
):
    steps = PARTS * nk
    width = lax.axis_index("width")
    hid = lax.axis_index("hidden")
    z = lax.rem(width, 4)
    yl = lax.div(width, 4)
    core = lax.rem(hid, 2)
    yh = lax.rem(lax.div(hid, 2), 2)
    x = lax.div(hid, 4)
    zp, zm, zq = lax.rem(z + 1, 4), lax.rem(z + 3, 4), lax.rem(z + 2, 4)
    xp, xm, xq = lax.rem(x + 1, 4), lax.rem(x + 3, 4), lax.rem(x + 2, 4)

    def at_z(to):
        return (yl * 4 + to, hid)

    def other_y(to):
        return ((1 - yl) * 4 + to, hid)

    def at_chip(its_x, its_yh):
        return (width, its_x * 4 + its_yh * 2 + core)

    def at_x(to):
        return at_chip(to, yh)

    partner = ((1 - yl) * 4 + z, hid)
    sibling = (width, hid + 1 - 2 * core)
    across = (width, x * 4 + (1 - yh) * 2 + core)

    def place(its_x, its_yh):
        return lax.rem(its_x * 2 + its_yh + 4 * yl, 8)

    def weight_copies(k):
        cols = pl.ds(k * COLS, COLS) if isinstance(k, int) else pl.ds(pl.multiple_of(k * COLS, COLS), COLS)
        return (
            pltpu.make_async_copy(gate_w.at[:, cols], wg.at[k], w_sem.at[0, k]),
            pltpu.make_async_copy(up_w.at[:, cols], wu.at[k], w_sem.at[1, k]),
            pltpu.make_async_copy(down_w.at[cols, :], wd.at[k], w_sem.at[2, k]),
        )

    pair = ((tokens, tok), (grad_out, grd))

    def own_copy(p, a):
        src, dst = pair[a]
        return pltpu.make_async_copy(
            src.at[pl.ds(p * PIECE, PIECE)], dst.at[p, place(x, yh), core], o_sem.at[a, p]
        )

    for p in range(PARTS):
        for a in range(2):
            own_copy(p, a).start()
    for copy in weight_copies(0):
        copy.start()

    barrier = pltpu.get_barrier_semaphore()
    friends = [at_z(zp), at_z(zm), at_z(zq), partner, other_y(zp), other_y(zm), other_y(zq), sibling, across]
    friends += [at_chip(to, its_yh) for to in (xp, xm, xq) for its_yh in (yh, 1 - yh)]
    for friend in friends:
        pl.semaphore_signal(barrier, inc=1, device_id=friend, device_id_type=MESH)
    pl.semaphore_wait(barrier, len(friends))

    def gathered(p, a, i):
        its_x = (x, x, xm, xp, xq, xm, xp, xq)[i if i < 8 else i - 7]
        its_yh = (yh, 1 - yh, yh, yh, yh, 1 - yh, 1 - yh, 1 - yh)[i if i < 8 else i - 7]
        its_core = core if 0 < i < 8 else 1 - core
        return pair[a][1].at[p, place(its_x, its_yh), its_core]

    def gather_copy(p, a, i):
        to = (sibling, across, at_x(xp), at_x(xm), at_x(xq), at_x(xp), at_x(xm), at_x(xq))
        if i < 5:
            src = dst = pair[a][1].at[p, place(x, yh), core]
        elif i < 8 and p == 0:
            src = dst = pair[a][1].at[p, place(x, yh), core]
        elif i < 8:
            src = dst = gathered(p, a, 1)
        else:
            src = dst = gathered(p, a, i - 7)
        if p == 0:
            to = to[:5] + (at_chip(xp, 1 - yh), at_chip(xm, 1 - yh), at_chip(xq, 1 - yh))
        return remote(src, dst, hs_sem.at[p, a, i], hr_sem.at[p, a, i], to[i] if i < 8 else sibling)

    def gather_arrived(p, a, i):
        dst = gathered(p, a, i)
        remote(dst, dst, hs_sem.at[p, a, i], hr_sem.at[p, a, i], sibling).wait_recv()

    def gather_early(p, a):
        own_copy(p, a).wait()
        gather_copy(p, a, 1).start()

    def gather_send(p, a):
        if p == 0:
            own_copy(p, a).wait()
        for i in (1, 5, 6, 7, 2, 3, 4, 0) if p == 0 else (2, 3, 4, 0):
            gather_copy(p, a, i).start()

    def gather_across(p, a):
        gather_arrived(p, a, 1)
        for i in (8,) if p == 0 else (5, 6, 7, 8):
            gather_copy(p, a, i).start()

    def gather_share(p, a):
        for i in range(2, 8):
            gather_arrived(p, a, i)
            gather_copy(p, a, i + 7).start()

    def gather_wait(p, a):
        for i in (0, *range(8, 15)):
            gather_arrived(p, a, i)

    for a in range(2):
        gather_send(0, a)
    for k in range(1, nk):
        for copy in weight_copies(k):
            copy.start()
    for p in range(1, PARTS):
        for a in range(2):
            gather_early(p, a)

    blocks = COLS // BLOCK
    for b in range(nk * blocks):
        lanes = slice((b % blocks) * BLOCK, (b % blocks + 1) * BLOCK)
        for pat, mask in ((pat_gate, mg), (pat_up, mu)):
            hit = jnp.where(pat[...] == hid * (nk * blocks) + b, 1.0, 0.0)
            hit = jnp.max(hit, axis=1, keepdims=True)
            mask[b // blocks, :, lanes] = jnp.broadcast_to(hit, (8, BLOCK))
    for b in range(8):
        hit = jnp.where(pat_down[...] == width * 8 + b, 1.0, 0.0)
        hit = jnp.max(hit, axis=1, keepdims=True)
        md[:, b * BLOCK:(b + 1) * BLOCK] = jnp.broadcast_to(hit, (nk * blocks, BLOCK))

    def split(s):
        return lax.div(s, nk), lax.rem(s, nk)

    rows = 16 * PIECE
    half, slot_rows = rows // 2, rows // 8

    def masked_weights(k):
        for copy in weight_copies(k):
            copy.wait()
        for r in range(8):
            at = slice(r * BLOCK, (r + 1) * BLOCK)
            for w, mask in ((wg, mg), (wu, mu)):
                keep = jnp.broadcast_to(mask[k, r:r + 1, :], (BLOCK, COLS)).astype(BF16)
                w[k, at, :] = w[k, at, :] * keep
        for i in range(blocks):
            at = slice(i * BLOCK, (i + 1) * BLOCK)
            row = md[pl.ds(blocks * k + i, 1), :]
            keep = jnp.broadcast_to(row, (BLOCK, row.shape[1])).astype(BF16)
            wd[k, at, :] = wd[k, at, :] * keep

    def z_copy(s, i):
        return remote(zsend.at[s, i], zrecv.at[s, i], zs_sem.at[s, i], zr_sem.at[s, i], at_z((zq, zp, zm)[i]))

    def straight_copy(i):
        to = (zq, zp, zm, z)[i]
        return remote(
            ysend.at[steps - 1, to], yrecv.at[steps - 1, z], yd_sem.at[i], yd_sem.at[4 + i], other_y(to)
        )

    def straight_wait(i):
        src = yrecv.at[steps - 1, (zq, zm, zp, z)[i]]
        remote(src, src, yd_sem.at[i], yd_sem.at[4 + i], partner).wait_recv()

    def first_copy(i):
        cols = (pl.ds(0, 2 * COLS), pl.ds(2 * COLS, COLS))[i]
        return remote(ysend.at[0, :, :, cols], yrecv.at[0, :, :, cols], y0_sem.at[i], y0_sem.at[2 + i], partner)

    def partials(s):
        part, k = split(s)
        slot = lax.rem(s, SLOTS)

        @pl.when(s < nk)
        def _():
            masked_weights(k)

        for p in range(1, PARTS):
            @pl.when(s == p * nk)
            def _():
                gather_wait(p, 0)
                gather_wait(p, 1)

        @pl.when(s == 0)
        def _():
            gather_across(0, 0)
            gather_share(0, 0)
            gather_wait(0, 0)

        def put(at, value):
            cols = slice(at * COLS, (at + 1) * COLS)
            own[slot, :, :, cols] = value[:half].reshape(4, slot_rows, COLS)
            ysend[s, :, :, cols] = value[half:].astype(BF16).reshape(4, slot_rows, COLS)

        t = tok[part].reshape(rows, -1)
        put(0, jnp.dot(t, wg[k], preferred_element_type=F32))
        put(1, jnp.dot(t, wu[k], preferred_element_type=F32))

        @pl.when(s == 0)
        def _():
            first_copy(0).start()
            gather_across(0, 1)
            gather_share(0, 1)
            gather_wait(0, 1)
        put(2, nt(grd[part].reshape(rows, -1), wd[k]))

        @pl.when(s == 0)
        def _():
            first_copy(1).start()

        @pl.when((s > 0) & (s < steps - 1))
        def _():
            remote(ysend.at[s], yrecv.at[s], ys_sem.at[s], yr_sem.at[s], partner).start()

        @pl.when(s == steps - 1)
        def _():
            for i in range(4):
                straight_copy(i).start()
            for i, to in enumerate((zq, zp, zm)):
                zsend[s, i] = own[slot, to].astype(BF16)
                z_copy(s, i).start()

        for p in range(1, PARTS):
            for at, what in ((0, gather_send), (2, gather_across), (4, gather_share)):
                @pl.when(s == (p - 1) * nk + at)
                def _():
                    what(p, 0)
                    what(p, 1)

    def pair_sum(s, at):
        return own[lax.rem(s, SLOTS), at] + yrecv[s, at].astype(F32)

    def after_pair(s):
        @pl.when(s == 0)
        def _():
            for i in range(2):
                first_copy(i).wait_recv()

        @pl.when((s > 0) & (s < steps - 1))
        def _():
            remote(ysend.at[s], yrecv.at[s], ys_sem.at[s], yr_sem.at[s], partner).wait_recv()

        @pl.when(s < steps - 1)
        def _():
            for i, to in enumerate((zq, zp, zm)):
                zsend[s, i] = pair_sum(s, to).astype(BF16)
                z_copy(s, i).start()

    def ag_copy(s, i):
        src, to = (
            ((0, z), at_z(zp)), ((0, z), at_z(zm)), ((0, z), partner),
            ((1, z), at_z(zp)), ((1, z), at_z(zm)),
            ((0, zp), at_z(zm)), ((1, zm), at_z(zp)),
        )[i]
        here = ag.at[s, src[0], src[1]]
        there = ag.at[s, 1, z] if i == 2 else here
        return remote(here, there, as_sem.at[s, i], ar_sem.at[s, i], to)

    def ag_direct(s, i):
        to = (other_y(zp), other_y(zm), at_z(zq), other_y(zq))[i - 3]
        there = ag.at[s, 0 if i == 5 else 1, z]
        return remote(ag.at[s, 0, z], there, as_sem.at[s, i], ar_sem.at[s, i], to)

    def ag_wait(s, i):
        y, at = ((0, zm), (0, zp), (1, z), (1, zm), (1, zp), (0, zq), (1, zq))[i]
        here = ag.at[s, y, at]
        remote(here, here, as_sem.at[s, i], ar_sem.at[s, i], partner).wait_recv()

    def activate(s):
        at = lax.rem(s, SLOTS)

        @pl.when(s == steps - 1)
        def _():
            for i in range(4):
                straight_wait(i)
            for to in (zq, zp, zm):
                own[at, z] += yrecv[s, to].astype(F32)
        for i in range(3):
            z_copy(s, i).wait_recv()
        total = pair_sum(s, z)
        for i in range(3):
            total = total + zrecv[s, i].astype(F32)
        gate, up, gh = total[:, :COLS], total[:, COLS:2 * COLS], total[:, 2 * COLS:]
        sig = 1.0 / (1.0 + jnp.exp(-gate))
        silu = gate * sig
        ag[s, 0, z, :, :COLS] = (silu * up).astype(BF16)
        ag[s, 0, z, :, COLS:2 * COLS] = (gh * up * sig * (1.0 + gate * (1.0 - sig))).astype(BF16)
        ag[s, 0, z, :, 2 * COLS:] = (gh * silu).astype(BF16)
        for i in (2, 0, 1):
            ag_copy(s, i).start()

        @pl.when(s >= steps - DIRECT)
        def _():
            for i in (3, 4, 5, 6):
                ag_direct(s, i).start()

    def pass_partner(s):
        ag_wait(s, 2)

        @pl.when(s < steps - DIRECT)
        def _():
            ag_copy(s, 3).start()
            ag_copy(s, 4).start()

    def pass_on(s):
        ag_wait(s, 1)

        @pl.when(s < steps - DIRECT)
        def _():
            ag_copy(s, 5).start()
        ag_wait(s, 3)

        @pl.when(s < steps - DIRECT)
        def _():
            ag_copy(s, 6).start()

    def back(s):
        part, k = split(s)
        slot = lax.rem(part, 2)
        for i in (0, 4, 5, 6):
            ag_wait(s, i)

        @pl.when(s == 2 * nk)
        def _():
            for i in range(8):
                tail_copy(0, i).wait_send()

        @pl.when(k == 0)
        def _():
            acc[slot] = jnp.zeros(acc.shape[1:], F32)

        hidden = ag[s, :, :, :, :COLS].reshape(rows, COLS)
        d_gate = ag[s, :, :, :, COLS:2 * COLS].reshape(rows, COLS)
        d_up = ag[s, :, :, :, 2 * COLS:].reshape(rows, COLS)
        for n in range(4):
            cols = slice(n * 256, (n + 1) * 256)
            acc[slot, 0, :, cols] += jnp.dot(hidden, wd[k, :, cols], preferred_element_type=F32)
            acc[slot, 1, :, cols] += nt(d_gate, wg[k, cols, :]) + nt(d_up, wu[k, cols, :])

    def tail_chip(i):
        return (xp, xm, xq, x)[i // 2], i % 2

    def tail_rows(i, its_core):
        return pl.ds(pl.multiple_of(place(*tail_chip(i)) * slot_rows + its_core * PIECE, PIECE), PIECE)

    def tail_copy(p, i):
        return remote(
            acc.at[p % 2, :, tail_rows(i, 1 - core), :], crecv.at[p, i], cs_sem.at[p, i], cr_sem.at[p, i], sibling
        )

    def tail_pair(p):
        for i in range(8):
            tail_copy(p, i).start()

    def core_sum(p, i):
        return acc[p % 2, :, tail_rows(i, core), :] + crecv[p, i]

    def x_copy(p, i):
        return remote(xsend.at[p, i], xrecv.at[p, i], xs_sem.at[p, i], xr_sem.at[p, i], at_x((xp, xm, xq)[i]))

    def tail_x(p):
        for i in range(8):
            tail_copy(p, i).wait_recv()
            if i < 6:
                xsend[p, i // 2, i % 2] = core_sum(p, i).astype(BF16)
                if i % 2 == 1:
                    x_copy(p, i // 2).start()

    def across_copy(p):
        return remote(fsend.at[p], frecv.at[p], fs_sem.at[p], fr_sem.at[p], across)

    def tail_y(p):
        for i in range(3):
            x_copy(p, i).wait_recv()
        for its_yh in range(2):
            total = core_sum(p, 6 + its_yh)
            for i in range(3):
                total = total + xrecv[p, i, its_yh].astype(F32)

            @pl.when(yh == its_yh)
            def _():
                kept[p] = total

            @pl.when(yh != its_yh)
            def _():
                fsend[p] = total.astype(BF16)
        across_copy(p).start()

    def tail_end(p):
        across_copy(p).wait_recv()
        at = slice(p * PIECE, (p + 1) * PIECE)
        output[at, :] = (kept[p, 0] + frecv[p, 0].astype(F32)).astype(BF16)
        grad_tokens[at, :] = (kept[p, 1] + frecv[p, 1].astype(F32)).astype(BF16)

    def last_copy(i):
        its_x, its_yh = ((xp, yh), (xm, yh), (xp, 1 - yh), (xm, 1 - yh), (xq, yh), (xq, 1 - yh), (x, 1 - yh))[i]
        return remote(lsend.at[i], lrecv.at[i], ls_sem.at[i], lr_sem.at[i], at_chip(its_x, its_yh))

    def last_slot(i):
        return ((0, yh), (1, yh), (0, 1 - yh), (1, 1 - yh), (2, yh), (2, 1 - yh), (3, 1 - yh), (3, yh))[i]

    def last_sum_of(i):
        its_x, its_yh = last_slot(i)
        place_x = (xp, xm, xq, x)[its_x]
        at = pl.ds(pl.multiple_of(place(place_x, its_yh) * slot_rows + core * PIECE, PIECE), PIECE)
        return acc[(PARTS - 1) % 2, :, at, :] + crecv[PARTS - 1, its_x * 2 + its_yh]

    def last_send():
        for i in range(8):
            tail_copy(PARTS - 1, i).wait_recv()
            if i % 2 == 1:
                for j in ((0, 2), (1, 3), (4, 5), (6,))[i // 2]:
                    lsend[j] = last_sum_of(j).astype(BF16)
                    last_copy(j).start()

    def last_sum():
        total = last_sum_of(7)
        for i in range(7):
            last_copy(i).wait_recv()
            total = total + lrecv[i].astype(F32)
        at = slice((PARTS - 1) * PIECE, PARTS * PIECE)
        output[at, :] = total[0].astype(BF16)
        grad_tokens[at, :] = total[1].astype(BF16)

    def grad_copies(k):
        cols = pl.ds(k * COLS, COLS) if isinstance(k, int) else pl.ds(pl.multiple_of(k * COLS, COLS), COLS)
        at = k % 2 if isinstance(k, int) else lax.rem(k, 2)
        return (
            pltpu.make_async_copy(gg.at[at], grad_gate.at[:, cols], g_sem.at[at, 0]),
            pltpu.make_async_copy(gu.at[at], grad_up.at[:, cols], g_sem.at[at, 1]),
            pltpu.make_async_copy(gd.at[at], grad_down.at[cols, :], g_sem.at[at, 2]),
        )

    def weight_grads(k):
        at = k % 2 if isinstance(k, int) else lax.rem(k, 2)

        @pl.when(k >= 2)
        def _():
            for copy in grad_copies(k - 2):
                copy.wait()

        def units(i):
            cols = slice(i * COLS, (i + 1) * COLS)
            return jnp.concatenate(
                [ag[p * nk + k, :, :, :, cols].reshape(rows, COLS) for p in range(PARTS)], axis=0
            )

        contract = (((0,), (0,)), ((), ()))
        hidden, d_gate, d_up = units(0), units(1), units(2)
        for n in range(4):
            cols = slice(n * 256, (n + 1) * 256)
            t = tok[:, :, :, :, cols].reshape(PARTS * rows, 256)
            for d, mask, out in ((d_gate, mg, gg), (d_up, mu, gu)):
                res = lax.dot_general(t, d, contract, preferred_element_type=F32)
                for r in range(2):
                    keep = jnp.broadcast_to(mask[k, 2 * n + r:2 * n + r + 1, :], (BLOCK, COLS))
                    kept_rows = jnp.where(keep > 0.0, res[r * BLOCK:(r + 1) * BLOCK], 0.0)
                    out[at, (2 * n + r) * BLOCK:(2 * n + r + 1) * BLOCK, :] = kept_rows.astype(BF16)
            g = grd[:, :, :, :, cols].reshape(PARTS * rows, 256)
            res = lax.dot_general(hidden, g, contract, preferred_element_type=F32)
            for i in range(blocks):
                row = md[pl.ds(blocks * k + i, 1), cols]
                keep = jnp.broadcast_to(row, (BLOCK, 256))
                kept_rows = jnp.where(keep > 0.0, res[i * BLOCK:(i + 1) * BLOCK], 0.0)
                gd[at, i * BLOCK:(i + 1) * BLOCK, cols] = kept_rows.astype(BF16)
        for copy in grad_copies(k):
            copy.start()

    lag = LAGS[-1]

    def step(t, carry):
        def run(offset, what):
            s = t - offset

            @pl.when((s >= 0) & (s < steps))
            def _():
                what(s)

        k = t - LAGS[-1] - 1 - (PARTS - 1) * nk

        @pl.when(k >= 0)
        def _():
            weight_grads(k)

        for offset, what in zip(LAGS, (partials, after_pair, activate, pass_partner, pass_on, back)):
            run(offset, what)

        for p in range(PARTS - 1):
            for after, what in enumerate((tail_pair, tail_x, tail_y, tail_end)):
                @pl.when(t == (p + 1) * nk - 1 + lag + after)
                def _():
                    what(p)
        return carry

    lax.fori_loop(0, steps + lag, step, 0)
    tail_pair(PARTS - 1)
    last_send()
    weight_grads(nk - 1)
    last_sum()

    def drain(s, carry):
        @pl.when((s > 0) & (s < steps - 1))
        def _():
            remote(ysend.at[s], yrecv.at[s], ys_sem.at[s], yr_sem.at[s], partner).wait_send()
        for i in range(3):
            z_copy(s, i).wait_send()
        for i in range(7):
            ag_copy(s, i).wait_send()
        return carry

    lax.fori_loop(0, steps, drain, 0)
    for i in range(2):
        first_copy(i).wait_send()
    for i in range(4):
        straight_copy(i).wait_send()
    for p in range(PARTS):
        for a in range(2):
            for i in range(15):
                gather_copy(p, a, i).wait_send()
        if p > 0:
            for i in range(8):
                tail_copy(p, i).wait_send()
        if p < PARTS - 1:
            for i in range(3):
                x_copy(p, i).wait_send()
            across_copy(p).wait_send()
    for i in range(7):
        last_copy(i).wait_send()
    for k in (nk - 2, nk - 1):
        for copy in grad_copies(k):
            copy.wait()


def layer(tokens, gate_w, up_w, down_w, grad_out, pat_gate, pat_up, pat_down):
    rows, width = tokens.shape
    hidden = gate_w.shape[1]
    nk = hidden // COLS
    steps = PARTS * nk
    any_, vmem = pl.BlockSpec(memory_space=pl.ANY), pl.BlockSpec(memory_space=pltpu.VMEM)
    dma, three, slot_rows = pltpu.SemaphoreType.DMA, 3 * COLS, 2 * PIECE
    small = jax.ShapeDtypeStruct((rows, width), BF16)
    whole = (PARTS, 8, 2, PIECE, width)
    return pl.pallas_call(
        functools.partial(layer_kernel, nk),
        name="layer",
        out_shape=(
            small, small,
            jax.ShapeDtypeStruct((width, hidden), BF16),
            jax.ShapeDtypeStruct((width, hidden), BF16),
            jax.ShapeDtypeStruct((hidden, width), BF16),
        ),
        in_specs=[any_] * 5 + [vmem] * 3,
        out_specs=(vmem, vmem, any_, any_, any_),
        scratch_shapes=[
            pltpu.VMEM((nk, width, COLS), BF16),
            pltpu.VMEM((nk, width, COLS), BF16),
            pltpu.VMEM((nk, COLS, width), BF16),
            pltpu.VMEM((nk, 8, COLS), F32),
            pltpu.VMEM((nk, 8, COLS), F32),
            pltpu.VMEM((hidden // BLOCK, width), F32),
            pltpu.VMEM(whole, BF16),
            pltpu.VMEM(whole, BF16),
            pltpu.VMEM((SLOTS, 4, slot_rows, three), F32),
            pltpu.VMEM((steps, 4, slot_rows, three), BF16),
            pltpu.VMEM((steps, 4, slot_rows, three), BF16),
            pltpu.VMEM((steps, 3, slot_rows, three), BF16),
            pltpu.VMEM((steps, 3, slot_rows, three), BF16),
            pltpu.VMEM((steps, 2, 4, slot_rows, three), BF16),
            pltpu.VMEM((2, 2, 16 * PIECE, width), F32),
            pltpu.VMEM((PARTS, 8, 2, PIECE, width), F32),
            pltpu.VMEM((PARTS, 3, 2, 2, PIECE, width), BF16),
            pltpu.VMEM((PARTS, 3, 2, 2, PIECE, width), BF16),
            pltpu.VMEM((PARTS, 2, PIECE, width), F32),
            pltpu.VMEM((PARTS, 2, PIECE, width), BF16),
            pltpu.VMEM((PARTS, 2, PIECE, width), BF16),
            pltpu.VMEM((2, width, COLS), BF16),
            pltpu.VMEM((2, width, COLS), BF16),
            pltpu.VMEM((2, COLS, width), BF16),
            pltpu.VMEM((7, 2, PIECE, width), BF16),
            pltpu.VMEM((7, 2, PIECE, width), BF16),
            dma((3, nk)), dma((2, PARTS)), dma((PARTS, 2, 15)), dma((PARTS, 2, 15)),
            dma((steps,)), dma((steps,)), dma((steps, 3)), dma((steps, 3)),
            dma((steps, 7)), dma((steps, 7)), dma((PARTS, 8)), dma((PARTS, 8)),
            dma((PARTS, 3)), dma((PARTS, 3)), dma((PARTS,)), dma((PARTS,)),
            dma((2, 3)), dma((7,)), dma((7,)), dma((4,)), dma((8,)),
        ],
        compiler_params=pltpu.CompilerParams(
            collective_id=0, has_side_effects=True, vmem_limit_bytes=60 * 2**20
        ),
    )(tokens, gate_w, up_w, down_w, grad_out, pat_gate, pat_up, pat_down)


def hand_out_kernel(*refs):
    n = (len(refs) - 2) // 3
    reads, writes = refs[-2:]
    pieces = []
    for a in range(n):
        src, dst, held = refs[a], refs[n + a], refs[2 * n + a]
        cuts = CUTS if src.shape[0] >= 256 else 1
        size = src.shape[0] // cuts
        for c in range(cuts):
            at = pl.ds(c * size, size)
            pieces.append((
                pltpu.make_async_copy(src.at[at], held.at[at], reads.at[a, c]),
                pltpu.make_async_copy(held.at[at], dst.at[at], writes.at[a, c]),
            ))
    for read, _ in pieces:
        read.start()
    for read, write in pieces:
        read.wait()
        write.start()
    for _, write in pieces:
        write.wait()


def hand_out(*arrays):
    any_ = pl.BlockSpec(memory_space=pl.ANY)
    n = len(arrays)
    return pl.pallas_call(
        hand_out_kernel,
        name="hand_out",
        out_shape=tuple(jax.ShapeDtypeStruct(a.shape, a.dtype) for a in arrays),
        in_specs=[any_] * n,
        out_specs=(any_,) * n,
        scratch_shapes=[pltpu.VMEM(a.shape, a.dtype) for a in arrays]
        + [pltpu.SemaphoreType.DMA((n, CUTS)), pltpu.SemaphoreType.DMA((n, CUTS))],
        compiler_params=pltpu.CompilerParams(vmem_limit_bytes=60 * 2**20),
        cost_estimate=pl.CostEstimate(
            flops=0, bytes_accessed=sum(4 * a.size for a in arrays), transcendentals=0
        ),
    )(*arrays)


def per_device(*args):
    return hand_out(*layer(*args))


def solution(mesh):
    placed = (
        P("hidden", "width"),
        P("width", "hidden"),
        P("width", "hidden"),
        P("hidden", "width"),
        P("hidden", "width"),
        P("width", None),
        P("width", None),
        P("hidden", None),
    )
    return jax.shard_map(
        per_device,
        mesh=mesh,
        in_specs=placed,
        out_specs=(
            P("hidden", "width"),
            P("hidden", "width"),
            P("width", "hidden"),
            P("width", "hidden"),
            P("hidden", "width"),
        ),
        check_vma=False,
    )
```

```python
import functools

import jax
import jax.numpy as jnp
from jax import lax
from jax.experimental import pallas as pl
from jax.experimental.pallas import tpu as pltpu
from jax.sharding import PartitionSpec as P

BLOCK = 128
COLS = 256
PARTS = 3
PIECE = 16
LAGS = (0, 1, 2, 3, 4, 5)
SLOTS = 4
LATE = 2
DIRECT = 1
CUTS = 4
MESH = pl.DeviceIdType.MESH
F32 = jnp.float32
BF16 = jnp.bfloat16


def remote(src, dst, send, recv, device):
    return pltpu.make_async_remote_copy(
        src_ref=src, dst_ref=dst, send_sem=send, recv_sem=recv,
        device_id=device, device_id_type=MESH,
    )


def nt(a, b):
    return lax.dot_general(a, b, (((1,), (1,)), ((), ())), preferred_element_type=F32)


def layer_kernel(
    nk,
    tokens, gate_w, up_w, down_w, grad_out, pat_gate, pat_up, pat_down,
    output, grad_tokens, grad_gate, grad_up, grad_down,
    wg, wu, wd, mg, mu, md, tok, grd, own, ysend, yrecv, zsend, zrecv, ag, acc,
    crecv, xsend, xrecv, kept, fsend, frecv, gg, gu, gd, lsend, lrecv,
    w_sem, o_sem, hs_sem, hr_sem, ys_sem, yr_sem, zs_sem, zr_sem,
    as_sem, ar_sem, cs_sem, cr_sem, xs_sem, xr_sem, fs_sem, fr_sem, g_sem, ls_sem, lr_sem, y0_sem, yd_sem,
):
    steps = PARTS * nk
    width = lax.axis_index("width")
    hid = lax.axis_index("hidden")
    z = lax.rem(width, 4)
    yl = lax.div(width, 4)
    core = lax.rem(hid, 2)
    yh = lax.rem(lax.div(hid, 2), 2)
    x = lax.div(hid, 4)
    zp, zm, zq = lax.rem(z + 1, 4), lax.rem(z + 3, 4), lax.rem(z + 2, 4)
    xp, xm, xq = lax.rem(x + 1, 4), lax.rem(x + 3, 4), lax.rem(x + 2, 4)

    def at_z(to):
        return (yl * 4 + to, hid)

    def other_y(to):
        return ((1 - yl) * 4 + to, hid)

    def at_chip(its_x, its_yh):
        return (width, its_x * 4 + its_yh * 2 + core)

    def at_x(to):
        return at_chip(to, yh)

    partner = ((1 - yl) * 4 + z, hid)
    sibling = (width, hid + 1 - 2 * core)
    across = (width, x * 4 + (1 - yh) * 2 + core)

    def place(its_x, its_yh):
        return lax.rem(its_x * 2 + its_yh + 4 * yl, 8)

    def weight_copies(k):
        cols = pl.ds(k * COLS, COLS) if isinstance(k, int) else pl.ds(pl.multiple_of(k * COLS, COLS), COLS)
        return (
            pltpu.make_async_copy(gate_w.at[:, cols], wg.at[k], w_sem.at[0, k]),
            pltpu.make_async_copy(up_w.at[:, cols], wu.at[k], w_sem.at[1, k]),
            pltpu.make_async_copy(down_w.at[cols, :], wd.at[k], w_sem.at[2, k]),
        )

    pair = ((tokens, tok), (grad_out, grd))

    def own_copy(p, a):
        src, dst = pair[a]
        return pltpu.make_async_copy(
            src.at[pl.ds(p * PIECE, PIECE)], dst.at[p, place(x, yh), core], o_sem.at[a, p]
        )

    for p in range(PARTS):
        for a in range(2):
            own_copy(p, a).start()
    for copy in weight_copies(0):
        copy.start()

    barrier = pltpu.get_barrier_semaphore()
    friends = [at_z(zp), at_z(zm), at_z(zq), partner, other_y(zp), other_y(zm), other_y(zq), sibling, across]
    friends += [at_chip(to, its_yh) for to in (xp, xm, xq) for its_yh in (yh, 1 - yh)]
    for friend in friends:
        pl.semaphore_signal(barrier, inc=1, device_id=friend, device_id_type=MESH)
    pl.semaphore_wait(barrier, len(friends))

    def gathered(p, a, i):
        its_x = (x, x, xm, xp, xq, xm, xp, xq)[i if i < 8 else i - 7]
        its_yh = (yh, 1 - yh, yh, yh, yh, 1 - yh, 1 - yh, 1 - yh)[i if i < 8 else i - 7]
        its_core = core if 0 < i < 8 else 1 - core
        return pair[a][1].at[p, place(its_x, its_yh), its_core]

    def gather_copy(p, a, i):
        to = (sibling, across, at_x(xp), at_x(xm), at_x(xq), at_x(xp), at_x(xm), at_x(xq))
        if i < 5:
            src = dst = pair[a][1].at[p, place(x, yh), core]
        elif i < 8 and p == 0:
            src = dst = pair[a][1].at[p, place(x, yh), core]
        elif i < 8:
            src = dst = gathered(p, a, 1)
        else:
            src = dst = gathered(p, a, i - 7)
        if p == 0:
            to = to[:5] + (at_chip(xp, 1 - yh), at_chip(xm, 1 - yh), at_chip(xq, 1 - yh))
        return remote(src, dst, hs_sem.at[p, a, i], hr_sem.at[p, a, i], to[i] if i < 8 else sibling)

    def gather_arrived(p, a, i):
        dst = gathered(p, a, i)
        remote(dst, dst, hs_sem.at[p, a, i], hr_sem.at[p, a, i], sibling).wait_recv()

    def gather_early(p, a):
        own_copy(p, a).wait()
        gather_copy(p, a, 1).start()

    def gather_send(p, a):
        if p == 0:
            own_copy(p, a).wait()
        for i in (1, 5, 6, 7, 2, 3, 4, 0) if p == 0 else (2, 3, 4, 0):
            gather_copy(p, a, i).start()

    def gather_across(p, a):
        gather_arrived(p, a, 1)
        for i in (8,) if p == 0 else (5, 6, 7, 8):
            gather_copy(p, a, i).start()

    def gather_share(p, a):
        for i in range(2, 8):
            gather_arrived(p, a, i)
            gather_copy(p, a, i + 7).start()

    def gather_wait(p, a):
        for i in (0, *range(8, 15)):
            gather_arrived(p, a, i)

    for a in range(2):
        gather_send(0, a)
    for k in range(1, nk):
        for copy in weight_copies(k):
            copy.start()
    for p in range(1, PARTS):
        for a in range(2):
            gather_early(p, a)

    blocks = COLS // BLOCK
    for b in range(nk * blocks):
        lanes = slice((b % blocks) * BLOCK, (b % blocks + 1) * BLOCK)
        for pat, mask in ((pat_gate, mg), (pat_up, mu)):
            hit = jnp.where(pat[...] == hid * (nk * blocks) + b, 1.0, 0.0)
            hit = jnp.max(hit, axis=1, keepdims=True)
            mask[b // blocks, :, lanes] = jnp.broadcast_to(hit, (8, BLOCK))
    for b in range(8):
        hit = jnp.where(pat_down[...] == width * 8 + b, 1.0, 0.0)
        hit = jnp.max(hit, axis=1, keepdims=True)
        md[:, b * BLOCK:(b + 1) * BLOCK] = jnp.broadcast_to(hit, (nk * blocks, BLOCK))

    def split(s):
        return lax.div(s, nk), lax.rem(s, nk)

    rows = 16 * PIECE
    half, slot_rows = rows // 2, rows // 8

    def masked_weights(k):
        for copy in weight_copies(k):
            copy.wait()
        for r in range(8):
            at = slice(r * BLOCK, (r + 1) * BLOCK)
            for w, mask in ((wg, mg), (wu, mu)):
                keep = jnp.broadcast_to(mask[k, r:r + 1, :], (BLOCK, COLS)).astype(BF16)
                w[k, at, :] = w[k, at, :] * keep
        for i in range(blocks):
            at = slice(i * BLOCK, (i + 1) * BLOCK)
            row = md[pl.ds(blocks * k + i, 1), :]
            keep = jnp.broadcast_to(row, (BLOCK, row.shape[1])).astype(BF16)
            wd[k, at, :] = wd[k, at, :] * keep

    def z_copy(s, i):
        return remote(zsend.at[s, i], zrecv.at[s, i], zs_sem.at[s, i], zr_sem.at[s, i], at_z((zq, zp, zm)[i]))

    def straight_copy(i):
        to = (zq, zp, zm, z)[i]
        return remote(
            ysend.at[steps - 1, to], yrecv.at[steps - 1, z], yd_sem.at[i], yd_sem.at[4 + i], other_y(to)
        )

    def straight_wait(i):
        src = yrecv.at[steps - 1, (zq, zm, zp, z)[i]]
        remote(src, src, yd_sem.at[i], yd_sem.at[4 + i], partner).wait_recv()

    def first_copy(i):
        cols = (pl.ds(0, 2 * COLS), pl.ds(2 * COLS, COLS))[i]
        return remote(ysend.at[0, :, :, cols], yrecv.at[0, :, :, cols], y0_sem.at[i], y0_sem.at[2 + i], partner)

    def partials(s):
        part, k = split(s)
        slot = lax.rem(s, SLOTS)

        @pl.when(s < nk)
        def _():
            masked_weights(k)

        for p in range(1, PARTS):
            @pl.when(s == p * nk)
            def _():
                gather_wait(p, 0)
                gather_wait(p, 1)

        @pl.when(s == 0)
        def _():
            gather_across(0, 0)
            gather_share(0, 0)
            gather_wait(0, 0)

        def put(at, value):
            cols = slice(at * COLS, (at + 1) * COLS)
            own[slot, :, :, cols] = value[:half].reshape(4, slot_rows, COLS)
            ysend[s, :, :, cols] = value[half:].astype(BF16).reshape(4, slot_rows, COLS)

        t = tok[part].reshape(rows, -1)
        put(0, jnp.dot(t, wg[k], preferred_element_type=F32))
        put(1, jnp.dot(t, wu[k], preferred_element_type=F32))

        @pl.when(s == 0)
        def _():
            first_copy(0).start()
            gather_across(0, 1)
            gather_share(0, 1)
            gather_wait(0, 1)
        put(2, nt(grd[part].reshape(rows, -1), wd[k]))

        @pl.when(s == 0)
        def _():
            first_copy(1).start()

        @pl.when((s > 0) & (s < steps - 1))
        def _():
            remote(ysend.at[s], yrecv.at[s], ys_sem.at[s], yr_sem.at[s], partner).start()

        @pl.when(s == steps - 1)
        def _():
            for i in range(4):
                straight_copy(i).start()
            for i, to in enumerate((zq, zp, zm)):
                zsend[s, i] = own[slot, to].astype(BF16)
                z_copy(s, i).start()

        for p in range(1, PARTS):
            for at, what in ((0, gather_send), (2, gather_across), (4, gather_share)):
                @pl.when(s == (p - 1) * nk + at)
                def _():
                    what(p, 0)
                    what(p, 1)

    def pair_sum(s, at):
        return own[lax.rem(s, SLOTS), at] + yrecv[s, at].astype(F32)

    def after_pair(s):
        @pl.when(s == 0)
        def _():
            for i in range(2):
                first_copy(i).wait_recv()

        @pl.when((s > 0) & (s < steps - 1))
        def _():
            remote(ysend.at[s], yrecv.at[s], ys_sem.at[s], yr_sem.at[s], partner).wait_recv()

        @pl.when(s < steps - 1)
        def _():
            for i, to in enumerate((zq, zp, zm)):
                zsend[s, i] = pair_sum(s, to).astype(BF16)
                z_copy(s, i).start()

    def ag_copy(s, i):
        src, to = (
            ((0, z), at_z(zp)), ((0, z), at_z(zm)), ((0, z), partner),
            ((1, z), at_z(zp)), ((1, z), at_z(zm)),
            ((0, zp), at_z(zm)), ((1, zm), at_z(zp)),
        )[i]
        here = ag.at[s, src[0], src[1]]
        there = ag.at[s, 1, z] if i == 2 else here
        return remote(here, there, as_sem.at[s, i], ar_sem.at[s, i], to)

    def ag_direct(s, i):
        to = (other_y(zp), other_y(zm), at_z(zq), other_y(zq))[i - 3]
        there = ag.at[s, 0 if i == 5 else 1, z]
        return remote(ag.at[s, 0, z], there, as_sem.at[s, i], ar_sem.at[s, i], to)

    def ag_wait(s, i):
        y, at = ((0, zm), (0, zp), (1, z), (1, zm), (1, zp), (0, zq), (1, zq))[i]
        here = ag.at[s, y, at]
        remote(here, here, as_sem.at[s, i], ar_sem.at[s, i], partner).wait_recv()

    def activate(s):
        at = lax.rem(s, SLOTS)

        @pl.when(s == steps - 1)
        def _():
            for i in range(4):
                straight_wait(i)
            for to in (zq, zp, zm):
                own[at, z] += yrecv[s, to].astype(F32)
        for i in range(3):
            z_copy(s, i).wait_recv()
        total = pair_sum(s, z)
        for i in range(3):
            total = total + zrecv[s, i].astype(F32)
        gate, up, gh = total[:, :COLS], total[:, COLS:2 * COLS], total[:, 2 * COLS:]
        sig = 1.0 / (1.0 + jnp.exp(-gate))
        silu = gate * sig
        ag[s, 0, z, :, :COLS] = (silu * up).astype(BF16)
        ag[s, 0, z, :, COLS:2 * COLS] = (gh * up * sig * (1.0 + gate * (1.0 - sig))).astype(BF16)
        ag[s, 0, z, :, 2 * COLS:] = (gh * silu).astype(BF16)
        for i in (2, 0, 1):
            ag_copy(s, i).start()

        @pl.when(s >= steps - DIRECT)
        def _():
            for i in (3, 4, 5, 6):
                ag_direct(s, i).start()

    def pass_partner(s):
        ag_wait(s, 2)

        @pl.when(s < steps - DIRECT)
        def _():
            ag_copy(s, 3).start()
            ag_copy(s, 4).start()

    def pass_on(s):
        ag_wait(s, 1)

        @pl.when(s < steps - DIRECT)
        def _():
            ag_copy(s, 5).start()
        ag_wait(s, 3)

        @pl.when(s < steps - DIRECT)
        def _():
            ag_copy(s, 6).start()

    def back(s):
        part, k = split(s)
        slot = lax.rem(part, 2)
        for i in (0, 4, 5, 6):
            ag_wait(s, i)

        @pl.when(s == 2 * nk)
        def _():
            for i in range(8):
                tail_copy(0, i).wait_send()

        @pl.when(k == 0)
        def _():
            acc[slot] = jnp.zeros(acc.shape[1:], F32)

        hidden = ag[s, :, :, :, :COLS].reshape(rows, COLS)
        d_gate = ag[s, :, :, :, COLS:2 * COLS].reshape(rows, COLS)
        d_up = ag[s, :, :, :, 2 * COLS:].reshape(rows, COLS)
        for n in range(4):
            cols = slice(n * 256, (n + 1) * 256)
            acc[slot, 0, :, cols] += jnp.dot(hidden, wd[k, :, cols], preferred_element_type=F32)
            acc[slot, 1, :, cols] += nt(d_gate, wg[k, cols, :]) + nt(d_up, wu[k, cols, :])

    def tail_chip(i):
        return (xp, xm, xq, x)[i // 2], i % 2

    def tail_rows(i, its_core):
        return pl.ds(pl.multiple_of(place(*tail_chip(i)) * slot_rows + its_core * PIECE, PIECE), PIECE)

    def tail_copy(p, i):
        return remote(
            acc.at[p % 2, :, tail_rows(i, 1 - core), :], crecv.at[p, i], cs_sem.at[p, i], cr_sem.at[p, i], sibling
        )

    def tail_pair(p):
        for i in range(8):
            tail_copy(p, i).start()

    def core_sum(p, i):
        return acc[p % 2, :, tail_rows(i, core), :] + crecv[p, i]

    def x_copy(p, i):
        return remote(xsend.at[p, i], xrecv.at[p, i], xs_sem.at[p, i], xr_sem.at[p, i], at_x((xp, xm, xq)[i]))

    def tail_x(p):
        for i in range(8):
            tail_copy(p, i).wait_recv()
            if i < 6:
                xsend[p, i // 2, i % 2] = core_sum(p, i).astype(BF16)
                if i % 2 == 1:
                    x_copy(p, i // 2).start()

    def across_copy(p):
        return remote(fsend.at[p], frecv.at[p], fs_sem.at[p], fr_sem.at[p], across)

    def tail_y(p):
        for i in range(3):
            x_copy(p, i).wait_recv()
        for its_yh in range(2):
            total = core_sum(p, 6 + its_yh)
            for i in range(3):
                total = total + xrecv[p, i, its_yh].astype(F32)

            @pl.when(yh == its_yh)
            def _():
                kept[p] = total

            @pl.when(yh != its_yh)
            def _():
                fsend[p] = total.astype(BF16)
        across_copy(p).start()

    def tail_end(p):
        across_copy(p).wait_recv()
        at = slice(p * PIECE, (p + 1) * PIECE)
        output[at, :] = (kept[p, 0] + frecv[p, 0].astype(F32)).astype(BF16)
        grad_tokens[at, :] = (kept[p, 1] + frecv[p, 1].astype(F32)).astype(BF16)

    def last_copy(i):
        its_x, its_yh = ((xp, yh), (xm, yh), (xp, 1 - yh), (xm, 1 - yh), (xq, yh), (xq, 1 - yh), (x, 1 - yh))[i]
        return remote(lsend.at[i], lrecv.at[i], ls_sem.at[i], lr_sem.at[i], at_chip(its_x, its_yh))

    def last_slot(i):
        return ((0, yh), (1, yh), (0, 1 - yh), (1, 1 - yh), (2, yh), (2, 1 - yh), (3, 1 - yh), (3, yh))[i]

    def last_sum_of(i):
        its_x, its_yh = last_slot(i)
        place_x = (xp, xm, xq, x)[its_x]
        at = pl.ds(pl.multiple_of(place(place_x, its_yh) * slot_rows + core * PIECE, PIECE), PIECE)
        return acc[(PARTS - 1) % 2, :, at, :] + crecv[PARTS - 1, its_x * 2 + its_yh]

    def last_send():
        for i in range(8):
            tail_copy(PARTS - 1, i).wait_recv()
            if i % 2 == 1:
                for j in ((0, 2), (1, 3), (4, 5), (6,))[i // 2]:
                    lsend[j] = last_sum_of(j).astype(BF16)
                    last_copy(j).start()

    def last_sum():
        total = last_sum_of(7)
        for i in range(7):
            last_copy(i).wait_recv()
            total = total + lrecv[i].astype(F32)
        at = slice((PARTS - 1) * PIECE, PARTS * PIECE)
        output[at, :] = total[0].astype(BF16)
        grad_tokens[at, :] = total[1].astype(BF16)

    def grad_copies(k):
        cols = pl.ds(k * COLS, COLS) if isinstance(k, int) else pl.ds(pl.multiple_of(k * COLS, COLS), COLS)
        at = k % 2 if isinstance(k, int) else lax.rem(k, 2)
        return (
            pltpu.make_async_copy(gg.at[at], grad_gate.at[:, cols], g_sem.at[at, 0]),
            pltpu.make_async_copy(gu.at[at], grad_up.at[:, cols], g_sem.at[at, 1]),
            pltpu.make_async_copy(gd.at[at], grad_down.at[cols, :], g_sem.at[at, 2]),
        )

    def weight_grads(k):
        at = k % 2 if isinstance(k, int) else lax.rem(k, 2)

        @pl.when(k >= 2)
        def _():
            for copy in grad_copies(k - 2):
                copy.wait()

        def units(i):
            cols = slice(i * COLS, (i + 1) * COLS)
            return jnp.concatenate(
                [ag[p * nk + k, :, :, :, cols].reshape(rows, COLS) for p in range(PARTS)], axis=0
            )

        contract = (((0,), (0,)), ((), ()))
        hidden, d_gate, d_up = units(0), units(1), units(2)
        for n in range(4):
            cols = slice(n * 256, (n + 1) * 256)
            t = tok[:, :, :, :, cols].reshape(PARTS * rows, 256)
            for d, mask, out in ((d_gate, mg, gg), (d_up, mu, gu)):
                res = lax.dot_general(t, d, contract, preferred_element_type=F32)
                for r in range(2):
                    keep = jnp.broadcast_to(mask[k, 2 * n + r:2 * n + r + 1, :], (BLOCK, COLS))
                    kept_rows = jnp.where(keep > 0.0, res[r * BLOCK:(r + 1) * BLOCK], 0.0)
                    out[at, (2 * n + r) * BLOCK:(2 * n + r + 1) * BLOCK, :] = kept_rows.astype(BF16)
            g = grd[:, :, :, :, cols].reshape(PARTS * rows, 256)
            res = lax.dot_general(hidden, g, contract, preferred_element_type=F32)
            for i in range(blocks):
                row = md[pl.ds(blocks * k + i, 1), cols]
                keep = jnp.broadcast_to(row, (BLOCK, 256))
                kept_rows = jnp.where(keep > 0.0, res[i * BLOCK:(i + 1) * BLOCK], 0.0)
                gd[at, i * BLOCK:(i + 1) * BLOCK, cols] = kept_rows.astype(BF16)
        for copy in grad_copies(k):
            copy.start()

    lag = LAGS[-1]

    def step(t, carry):
        def run(offset, what):
            s = t - offset

            @pl.when((s >= 0) & (s < steps))
            def _():
                what(s)

        k = t - LAGS[-1] - 1 - (PARTS - 1) * nk

        @pl.when((k >= 0) & (k < nk - LATE))
        def _():
            weight_grads(k)

        for offset, what in zip(LAGS, (partials, after_pair, activate, pass_partner, pass_on, back)):
            run(offset, what)

        for p in range(PARTS - 1):
            for after, what in enumerate((tail_pair, tail_x, tail_y, tail_end)):
                @pl.when(t == (p + 1) * nk - 1 + lag + after)
                def _():
                    what(p)
        return carry

    lax.fori_loop(0, steps + lag, step, 0)
    tail_pair(PARTS - 1)
    last_send()
    for k in range(nk - LATE, nk):
        weight_grads(k)
    last_sum()

    def drain(s, carry):
        @pl.when((s > 0) & (s < steps - 1))
        def _():
            remote(ysend.at[s], yrecv.at[s], ys_sem.at[s], yr_sem.at[s], partner).wait_send()
        for i in range(3):
            z_copy(s, i).wait_send()
        for i in range(7):
            ag_copy(s, i).wait_send()
        return carry

    lax.fori_loop(0, steps, drain, 0)
    for i in range(2):
        first_copy(i).wait_send()
    for i in range(4):
        straight_copy(i).wait_send()
    for p in range(PARTS):
        for a in range(2):
            for i in range(15):
                gather_copy(p, a, i).wait_send()
        if p > 0:
            for i in range(8):
                tail_copy(p, i).wait_send()
        if p < PARTS - 1:
            for i in range(3):
                x_copy(p, i).wait_send()
            across_copy(p).wait_send()
    for i in range(7):
        last_copy(i).wait_send()
    for k in (nk - 2, nk - 1):
        for copy in grad_copies(k):
            copy.wait()


def layer(tokens, gate_w, up_w, down_w, grad_out, pat_gate, pat_up, pat_down):
    rows, width = tokens.shape
    hidden = gate_w.shape[1]
    nk = hidden // COLS
    steps = PARTS * nk
    any_, vmem = pl.BlockSpec(memory_space=pl.ANY), pl.BlockSpec(memory_space=pltpu.VMEM)
    dma, three, slot_rows = pltpu.SemaphoreType.DMA, 3 * COLS, 2 * PIECE
    small = jax.ShapeDtypeStruct((rows, width), BF16)
    whole = (PARTS, 8, 2, PIECE, width)
    return pl.pallas_call(
        functools.partial(layer_kernel, nk),
        name="layer",
        out_shape=(
            small, small,
            jax.ShapeDtypeStruct((width, hidden), BF16),
            jax.ShapeDtypeStruct((width, hidden), BF16),
            jax.ShapeDtypeStruct((hidden, width), BF16),
        ),
        in_specs=[any_] * 5 + [vmem] * 3,
        out_specs=(vmem, vmem, any_, any_, any_),
        scratch_shapes=[
            pltpu.VMEM((nk, width, COLS), BF16),
            pltpu.VMEM((nk, width, COLS), BF16),
            pltpu.VMEM((nk, COLS, width), BF16),
            pltpu.VMEM((nk, 8, COLS), F32),
            pltpu.VMEM((nk, 8, COLS), F32),
            pltpu.VMEM((hidden // BLOCK, width), F32),
            pltpu.VMEM(whole, BF16),
            pltpu.VMEM(whole, BF16),
            pltpu.VMEM((SLOTS, 4, slot_rows, three), F32),
            pltpu.VMEM((steps, 4, slot_rows, three), BF16),
            pltpu.VMEM((steps, 4, slot_rows, three), BF16),
            pltpu.VMEM((steps, 3, slot_rows, three), BF16),
            pltpu.VMEM((steps, 3, slot_rows, three), BF16),
            pltpu.VMEM((steps, 2, 4, slot_rows, three), BF16),
            pltpu.VMEM((2, 2, 16 * PIECE, width), F32),
            pltpu.VMEM((PARTS, 8, 2, PIECE, width), F32),
            pltpu.VMEM((PARTS, 3, 2, 2, PIECE, width), BF16),
            pltpu.VMEM((PARTS, 3, 2, 2, PIECE, width), BF16),
            pltpu.VMEM((PARTS, 2, PIECE, width), F32),
            pltpu.VMEM((PARTS, 2, PIECE, width), BF16),
            pltpu.VMEM((PARTS, 2, PIECE, width), BF16),
            pltpu.VMEM((2, width, COLS), BF16),
            pltpu.VMEM((2, width, COLS), BF16),
            pltpu.VMEM((2, COLS, width), BF16),
            pltpu.VMEM((7, 2, PIECE, width), BF16),
            pltpu.VMEM((7, 2, PIECE, width), BF16),
            dma((3, nk)), dma((2, PARTS)), dma((PARTS, 2, 15)), dma((PARTS, 2, 15)),
            dma((steps,)), dma((steps,)), dma((steps, 3)), dma((steps, 3)),
            dma((steps, 7)), dma((steps, 7)), dma((PARTS, 8)), dma((PARTS, 8)),
            dma((PARTS, 3)), dma((PARTS, 3)), dma((PARTS,)), dma((PARTS,)),
            dma((2, 3)), dma((7,)), dma((7,)), dma((4,)), dma((8,)),
        ],
        compiler_params=pltpu.CompilerParams(
            collective_id=0, has_side_effects=True, vmem_limit_bytes=60 * 2**20
        ),
    )(tokens, gate_w, up_w, down_w, grad_out, pat_gate, pat_up, pat_down)


def hand_out_kernel(*refs):
    n = (len(refs) - 2) // 3
    reads, writes = refs[-2:]
    pieces = []
    for a in range(n):
        src, dst, held = refs[a], refs[n + a], refs[2 * n + a]
        cuts = CUTS if src.shape[0] >= 256 else 1
        size = src.shape[0] // cuts
        for c in range(cuts):
            at = pl.ds(c * size, size)
            pieces.append((
                pltpu.make_async_copy(src.at[at], held.at[at], reads.at[a, c]),
                pltpu.make_async_copy(held.at[at], dst.at[at], writes.at[a, c]),
            ))
    for read, _ in pieces:
        read.start()
    for read, write in pieces:
        read.wait()
        write.start()
    for _, write in pieces:
        write.wait()


def hand_out(*arrays):
    any_ = pl.BlockSpec(memory_space=pl.ANY)
    n = len(arrays)
    return pl.pallas_call(
        hand_out_kernel,
        name="hand_out",
        out_shape=tuple(jax.ShapeDtypeStruct(a.shape, a.dtype) for a in arrays),
        in_specs=[any_] * n,
        out_specs=(any_,) * n,
        scratch_shapes=[pltpu.VMEM(a.shape, a.dtype) for a in arrays]
        + [pltpu.SemaphoreType.DMA((n, CUTS)), pltpu.SemaphoreType.DMA((n, CUTS))],
        compiler_params=pltpu.CompilerParams(vmem_limit_bytes=60 * 2**20),
        cost_estimate=pl.CostEstimate(
            flops=0, bytes_accessed=sum(4 * a.size for a in arrays), transcendentals=0
        ),
    )(*arrays)


def per_device(*args):
    return hand_out(*layer(*args))


def solution(mesh):
    placed = (
        P("hidden", "width"),
        P("width", "hidden"),
        P("width", "hidden"),
        P("hidden", "width"),
        P("hidden", "width"),
        P("width", None),
        P("width", None),
        P("hidden", None),
    )
    return jax.shard_map(
        per_device,
        mesh=mesh,
        in_specs=placed,
        out_specs=(
            P("hidden", "width"),
            P("hidden", "width"),
            P("width", "hidden"),
            P("width", "hidden"),
            P("hidden", "width"),
        ),
        check_vma=False,
    )
```

```python
import functools

import jax
import jax.numpy as jnp
from jax import lax
from jax.experimental import pallas as pl
from jax.experimental.pallas import tpu as pltpu
from jax.sharding import PartitionSpec as P

BLOCK = 128
COLS = 256
PARTS = 3
PIECE = 16
LAGS = (0, 1, 2, 3, 4, 5)
SLOTS = 4
LATE = 2
DIRECT = 1
CUTS = 2
MESH = pl.DeviceIdType.MESH
F32 = jnp.float32
BF16 = jnp.bfloat16


def remote(src, dst, send, recv, device):
    return pltpu.make_async_remote_copy(
        src_ref=src, dst_ref=dst, send_sem=send, recv_sem=recv,
        device_id=device, device_id_type=MESH,
    )


def nt(a, b):
    return lax.dot_general(a, b, (((1,), (1,)), ((), ())), preferred_element_type=F32)


def layer_kernel(
    nk,
    tokens, gate_w, up_w, down_w, grad_out, pat_gate, pat_up, pat_down,
    output, grad_tokens, grad_gate, grad_up, grad_down,
    wg, wu, wd, mg, mu, md, tok, grd, own, ysend, yrecv, zsend, zrecv, ag, acc,
    crecv, xsend, xrecv, kept, fsend, frecv, gg, gu, gd, lsend, lrecv,
    w_sem, o_sem, hs_sem, hr_sem, ys_sem, yr_sem, zs_sem, zr_sem,
    as_sem, ar_sem, cs_sem, cr_sem, xs_sem, xr_sem, fs_sem, fr_sem, g_sem, ls_sem, lr_sem, y0_sem, yd_sem,
):
    steps = PARTS * nk
    width = lax.axis_index("width")
    hid = lax.axis_index("hidden")
    z = lax.rem(width, 4)
    yl = lax.div(width, 4)
    core = lax.rem(hid, 2)
    yh = lax.rem(lax.div(hid, 2), 2)
    x = lax.div(hid, 4)
    zp, zm, zq = lax.rem(z + 1, 4), lax.rem(z + 3, 4), lax.rem(z + 2, 4)
    xp, xm, xq = lax.rem(x + 1, 4), lax.rem(x + 3, 4), lax.rem(x + 2, 4)

    def at_z(to):
        return (yl * 4 + to, hid)

    def other_y(to):
        return ((1 - yl) * 4 + to, hid)

    def at_chip(its_x, its_yh):
        return (width, its_x * 4 + its_yh * 2 + core)

    def at_x(to):
        return at_chip(to, yh)

    partner = ((1 - yl) * 4 + z, hid)
    sibling = (width, hid + 1 - 2 * core)
    across = (width, x * 4 + (1 - yh) * 2 + core)

    def place(its_x, its_yh):
        return lax.rem(its_x * 2 + its_yh + 4 * yl, 8)

    def weight_copies(k):
        cols = pl.ds(k * COLS, COLS) if isinstance(k, int) else pl.ds(pl.multiple_of(k * COLS, COLS), COLS)
        return (
            pltpu.make_async_copy(gate_w.at[:, cols], wg.at[k], w_sem.at[0, k]),
            pltpu.make_async_copy(up_w.at[:, cols], wu.at[k], w_sem.at[1, k]),
            pltpu.make_async_copy(down_w.at[cols, :], wd.at[k], w_sem.at[2, k]),
        )

    pair = ((tokens, tok), (grad_out, grd))

    def own_copy(p, a):
        src, dst = pair[a]
        return pltpu.make_async_copy(
            src.at[pl.ds(p * PIECE, PIECE)], dst.at[p, place(x, yh), core], o_sem.at[a, p]
        )

    for p in range(PARTS):
        for a in range(2):
            own_copy(p, a).start()
    for copy in weight_copies(0):
        copy.start()

    barrier = pltpu.get_barrier_semaphore()
    friends = [at_z(zp), at_z(zm), at_z(zq), partner, other_y(zp), other_y(zm), other_y(zq), sibling, across]
    friends += [at_chip(to, its_yh) for to in (xp, xm, xq) for its_yh in (yh, 1 - yh)]
    for friend in friends:
        pl.semaphore_signal(barrier, inc=1, device_id=friend, device_id_type=MESH)
    pl.semaphore_wait(barrier, len(friends))

    def gathered(p, a, i):
        its_x = (x, x, xm, xp, xq, xm, xp, xq)[i if i < 8 else i - 7]
        its_yh = (yh, 1 - yh, yh, yh, yh, 1 - yh, 1 - yh, 1 - yh)[i if i < 8 else i - 7]
        its_core = core if 0 < i < 8 else 1 - core
        return pair[a][1].at[p, place(its_x, its_yh), its_core]

    def gather_copy(p, a, i):
        to = (sibling, across, at_x(xp), at_x(xm), at_x(xq), at_x(xp), at_x(xm), at_x(xq))
        if i < 5:
            src = dst = pair[a][1].at[p, place(x, yh), core]
        elif i < 8 and p == 0:
            src = dst = pair[a][1].at[p, place(x, yh), core]
        elif i < 8:
            src = dst = gathered(p, a, 1)
        else:
            src = dst = gathered(p, a, i - 7)
        if p == 0:
            to = to[:5] + (at_chip(xp, 1 - yh), at_chip(xm, 1 - yh), at_chip(xq, 1 - yh))
        return remote(src, dst, hs_sem.at[p, a, i], hr_sem.at[p, a, i], to[i] if i < 8 else sibling)

    def gather_arrived(p, a, i):
        dst = gathered(p, a, i)
        remote(dst, dst, hs_sem.at[p, a, i], hr_sem.at[p, a, i], sibling).wait_recv()

    def gather_early(p, a):
        own_copy(p, a).wait()
        gather_copy(p, a, 1).start()

    def gather_send(p, a):
        if p == 0:
            own_copy(p, a).wait()
        for i in (1, 5, 6, 7, 2, 3, 4, 0) if p == 0 else (2, 3, 4, 0):
            gather_copy(p, a, i).start()

    def gather_across(p, a):
        gather_arrived(p, a, 1)
        for i in (8,) if p == 0 else (5, 6, 7, 8):
            gather_copy(p, a, i).start()

    def gather_share(p, a):
        for i in range(2, 8):
            gather_arrived(p, a, i)
            gather_copy(p, a, i + 7).start()

    def gather_wait(p, a):
        for i in (0, *range(8, 15)):
            gather_arrived(p, a, i)

    for a in range(2):
        gather_send(0, a)
    for k in range(1, nk):
        for copy in weight_copies(k):
            copy.start()
    for p in range(1, PARTS):
        for a in range(2):
            gather_early(p, a)

    blocks = COLS // BLOCK
    for b in range(nk * blocks):
        lanes = slice((b % blocks) * BLOCK, (b % blocks + 1) * BLOCK)
        for pat, mask in ((pat_gate, mg), (pat_up, mu)):
            hit = jnp.where(pat[...] == hid * (nk * blocks) + b, 1.0, 0.0)
            hit = jnp.max(hit, axis=1, keepdims=True)
            mask[b // blocks, :, lanes] = jnp.broadcast_to(hit, (8, BLOCK))
    for b in range(8):
        hit = jnp.where(pat_down[...] == width * 8 + b, 1.0, 0.0)
        hit = jnp.max(hit, axis=1, keepdims=True)
        md[:, b * BLOCK:(b + 1) * BLOCK] = jnp.broadcast_to(hit, (nk * blocks, BLOCK))

    def split(s):
        return lax.div(s, nk), lax.rem(s, nk)

    rows = 16 * PIECE
    half, slot_rows = rows // 2, rows // 8

    def masked_weights(k):
        for copy in weight_copies(k):
            copy.wait()
        for r in range(8):
            at = slice(r * BLOCK, (r + 1) * BLOCK)
            for w, mask in ((wg, mg), (wu, mu)):
                keep = jnp.broadcast_to(mask[k, r:r + 1, :], (BLOCK, COLS)).astype(BF16)
                w[k, at, :] = w[k, at, :] * keep
        for i in range(blocks):
            at = slice(i * BLOCK, (i + 1) * BLOCK)
            row = md[pl.ds(blocks * k + i, 1), :]
            keep = jnp.broadcast_to(row, (BLOCK, row.shape[1])).astype(BF16)
            wd[k, at, :] = wd[k, at, :] * keep

    def z_copy(s, i):
        return remote(zsend.at[s, i], zrecv.at[s, i], zs_sem.at[s, i], zr_sem.at[s, i], at_z((zq, zp, zm)[i]))

    def straight_copy(i):
        to = (zq, zp, zm, z)[i]
        return remote(
            ysend.at[steps - 1, to], yrecv.at[steps - 1, z], yd_sem.at[i], yd_sem.at[4 + i], other_y(to)
        )

    def straight_wait(i):
        src = yrecv.at[steps - 1, (zq, zm, zp, z)[i]]
        remote(src, src, yd_sem.at[i], yd_sem.at[4 + i], partner).wait_recv()

    def first_copy(i):
        cols = (pl.ds(0, 2 * COLS), pl.ds(2 * COLS, COLS))[i]
        return remote(ysend.at[0, :, :, cols], yrecv.at[0, :, :, cols], y0_sem.at[i], y0_sem.at[2 + i], partner)

    def partials(s):
        part, k = split(s)
        slot = lax.rem(s, SLOTS)

        @pl.when(s < nk)
        def _():
            masked_weights(k)

        for p in range(1, PARTS):
            @pl.when(s == p * nk)
            def _():
                gather_wait(p, 0)
                gather_wait(p, 1)

        @pl.when(s == 0)
        def _():
            gather_across(0, 0)
            gather_share(0, 0)
            gather_wait(0, 0)

        def put(at, value):
            cols = slice(at * COLS, (at + 1) * COLS)
            own[slot, :, :, cols] = value[:half].reshape(4, slot_rows, COLS)
            ysend[s, :, :, cols] = value[half:].astype(BF16).reshape(4, slot_rows, COLS)

        t = tok[part].reshape(rows, -1)
        put(0, jnp.dot(t, wg[k], preferred_element_type=F32))
        put(1, jnp.dot(t, wu[k], preferred_element_type=F32))

        @pl.when(s == 0)
        def _():
            first_copy(0).start()
            gather_across(0, 1)
            gather_share(0, 1)
            gather_wait(0, 1)
        put(2, nt(grd[part].reshape(rows, -1), wd[k]))

        @pl.when(s == 0)
        def _():
            first_copy(1).start()

        @pl.when((s > 0) & (s < steps - 1))
        def _():
            remote(ysend.at[s], yrecv.at[s], ys_sem.at[s], yr_sem.at[s], partner).start()

        @pl.when(s == steps - 1)
        def _():
            for i in range(4):
                straight_copy(i).start()
            for i, to in enumerate((zq, zp, zm)):
                zsend[s, i] = own[slot, to].astype(BF16)
                z_copy(s, i).start()

        for p in range(1, PARTS):
            for at, what in ((0, gather_send), (2, gather_across), (4, gather_share)):
                @pl.when(s == (p - 1) * nk + at)
                def _():
                    what(p, 0)
                    what(p, 1)

    def pair_sum(s, at):
        return own[lax.rem(s, SLOTS), at] + yrecv[s, at].astype(F32)

    def after_pair(s):
        @pl.when(s == 0)
        def _():
            for i in range(2):
                first_copy(i).wait_recv()

        @pl.when((s > 0) & (s < steps - 1))
        def _():
            remote(ysend.at[s], yrecv.at[s], ys_sem.at[s], yr_sem.at[s], partner).wait_recv()

        @pl.when(s < steps - 1)
        def _():
            for i, to in enumerate((zq, zp, zm)):
                zsend[s, i] = pair_sum(s, to).astype(BF16)
                z_copy(s, i).start()

    def ag_copy(s, i):
        src, to = (
            ((0, z), at_z(zp)), ((0, z), at_z(zm)), ((0, z), partner),
            ((1, z), at_z(zp)), ((1, z), at_z(zm)),
            ((0, zp), at_z(zm)), ((1, zm), at_z(zp)),
        )[i]
        here = ag.at[s, src[0], src[1]]
        there = ag.at[s, 1, z] if i == 2 else here
        return remote(here, there, as_sem.at[s, i], ar_sem.at[s, i], to)

    def ag_direct(s, i):
        to = (other_y(zp), other_y(zm), at_z(zq), other_y(zq))[i - 3]
        there = ag.at[s, 0 if i == 5 else 1, z]
        return remote(ag.at[s, 0, z], there, as_sem.at[s, i], ar_sem.at[s, i], to)

    def ag_wait(s, i):
        y, at = ((0, zm), (0, zp), (1, z), (1, zm), (1, zp), (0, zq), (1, zq))[i]
        here = ag.at[s, y, at]
        remote(here, here, as_sem.at[s, i], ar_sem.at[s, i], partner).wait_recv()

    def activate(s):
        at = lax.rem(s, SLOTS)

        @pl.when(s == steps - 1)
        def _():
            for i in range(4):
                straight_wait(i)
            for to in (zq, zp, zm):
                own[at, z] += yrecv[s, to].astype(F32)
        for i in range(3):
            z_copy(s, i).wait_recv()
        total = pair_sum(s, z)
        for i in range(3):
            total = total + zrecv[s, i].astype(F32)
        gate, up, gh = total[:, :COLS], total[:, COLS:2 * COLS], total[:, 2 * COLS:]
        sig = 1.0 / (1.0 + jnp.exp(-gate))
        silu = gate * sig
        ag[s, 0, z, :, :COLS] = (silu * up).astype(BF16)
        ag[s, 0, z, :, COLS:2 * COLS] = (gh * up * sig * (1.0 + gate * (1.0 - sig))).astype(BF16)
        ag[s, 0, z, :, 2 * COLS:] = (gh * silu).astype(BF16)
        for i in (2, 0, 1):
            ag_copy(s, i).start()

        @pl.when(s >= steps - DIRECT)
        def _():
            for i in (3, 4, 5, 6):
                ag_direct(s, i).start()

    def pass_partner(s):
        ag_wait(s, 2)

        @pl.when(s < steps - DIRECT)
        def _():
            ag_copy(s, 3).start()
            ag_copy(s, 4).start()

    def pass_on(s):
        ag_wait(s, 1)

        @pl.when(s < steps - DIRECT)
        def _():
            ag_copy(s, 5).start()
        ag_wait(s, 3)

        @pl.when(s < steps - DIRECT)
        def _():
            ag_copy(s, 6).start()

    def back(s):
        part, k = split(s)
        slot = lax.rem(part, 2)
        for i in (0, 4, 5, 6):
            ag_wait(s, i)

        @pl.when(s == 2 * nk)
        def _():
            for i in range(8):
                tail_copy(0, i).wait_send()

        @pl.when(k == 0)
        def _():
            acc[slot] = jnp.zeros(acc.shape[1:], F32)

        hidden = ag[s, :, :, :, :COLS].reshape(rows, COLS)
        d_gate = ag[s, :, :, :, COLS:2 * COLS].reshape(rows, COLS)
        d_up = ag[s, :, :, :, 2 * COLS:].reshape(rows, COLS)
        for n in range(4):
            cols = slice(n * 256, (n + 1) * 256)
            acc[slot, 0, :, cols] += jnp.dot(hidden, wd[k, :, cols], preferred_element_type=F32)
            acc[slot, 1, :, cols] += nt(d_gate, wg[k, cols, :]) + nt(d_up, wu[k, cols, :])

    def tail_chip(i):
        return (xp, xm, xq, x)[i // 2], i % 2

    def tail_rows(i, its_core):
        return pl.ds(pl.multiple_of(place(*tail_chip(i)) * slot_rows + its_core * PIECE, PIECE), PIECE)

    def tail_copy(p, i):
        return remote(
            acc.at[p % 2, :, tail_rows(i, 1 - core), :], crecv.at[p, i], cs_sem.at[p, i], cr_sem.at[p, i], sibling
        )

    def tail_pair(p):
        for i in range(8):
            tail_copy(p, i).start()

    def core_sum(p, i):
        return acc[p % 2, :, tail_rows(i, core), :] + crecv[p, i]

    def x_copy(p, i):
        return remote(xsend.at[p, i], xrecv.at[p, i], xs_sem.at[p, i], xr_sem.at[p, i], at_x((xp, xm, xq)[i]))

    def tail_x(p):
        for i in range(8):
            tail_copy(p, i).wait_recv()
            if i < 6:
                xsend[p, i // 2, i % 2] = core_sum(p, i).astype(BF16)
                if i % 2 == 1:
                    x_copy(p, i // 2).start()

    def across_copy(p):
        return remote(fsend.at[p], frecv.at[p], fs_sem.at[p], fr_sem.at[p], across)

    def tail_y(p):
        for i in range(3):
            x_copy(p, i).wait_recv()
        for its_yh in range(2):
            total = core_sum(p, 6 + its_yh)
            for i in range(3):
                total = total + xrecv[p, i, its_yh].astype(F32)

            @pl.when(yh == its_yh)
            def _():
                kept[p] = total

            @pl.when(yh != its_yh)
            def _():
                fsend[p] = total.astype(BF16)
        across_copy(p).start()

    def tail_end(p):
        across_copy(p).wait_recv()
        at = slice(p * PIECE, (p + 1) * PIECE)
        output[at, :] = (kept[p, 0] + frecv[p, 0].astype(F32)).astype(BF16)
        grad_tokens[at, :] = (kept[p, 1] + frecv[p, 1].astype(F32)).astype(BF16)

    def last_copy(i):
        its_x, its_yh = ((xp, yh), (xm, yh), (xp, 1 - yh), (xm, 1 - yh), (xq, yh), (xq, 1 - yh), (x, 1 - yh))[i]
        return remote(lsend.at[i], lrecv.at[i], ls_sem.at[i], lr_sem.at[i], at_chip(its_x, its_yh))

    def last_slot(i):
        return ((0, yh), (1, yh), (0, 1 - yh), (1, 1 - yh), (2, yh), (2, 1 - yh), (3, 1 - yh), (3, yh))[i]

    def last_sum_of(i):
        its_x, its_yh = last_slot(i)
        place_x = (xp, xm, xq, x)[its_x]
        at = pl.ds(pl.multiple_of(place(place_x, its_yh) * slot_rows + core * PIECE, PIECE), PIECE)
        return acc[(PARTS - 1) % 2, :, at, :] + crecv[PARTS - 1, its_x * 2 + its_yh]

    def last_send():
        for i in range(8):
            tail_copy(PARTS - 1, i).wait_recv()
            if i % 2 == 1:
                for j in ((0, 2), (1, 3), (4, 5), (6,))[i // 2]:
                    lsend[j] = last_sum_of(j).astype(BF16)
                    last_copy(j).start()

    def last_sum():
        total = last_sum_of(7)
        for i in range(7):
            last_copy(i).wait_recv()
            total = total + lrecv[i].astype(F32)
        at = slice((PARTS - 1) * PIECE, PARTS * PIECE)
        output[at, :] = total[0].astype(BF16)
        grad_tokens[at, :] = total[1].astype(BF16)

    def grad_copies(k):
        cols = pl.ds(k * COLS, COLS) if isinstance(k, int) else pl.ds(pl.multiple_of(k * COLS, COLS), COLS)
        at = k % 2 if isinstance(k, int) else lax.rem(k, 2)
        return (
            pltpu.make_async_copy(gg.at[at], grad_gate.at[:, cols], g_sem.at[at, 0]),
            pltpu.make_async_copy(gu.at[at], grad_up.at[:, cols], g_sem.at[at, 1]),
            pltpu.make_async_copy(gd.at[at], grad_down.at[cols, :], g_sem.at[at, 2]),
        )

    def weight_grads(k):
        at = k % 2 if isinstance(k, int) else lax.rem(k, 2)

        @pl.when(k >= 2)
        def _():
            for copy in grad_copies(k - 2):
                copy.wait()

        def units(i):
            cols = slice(i * COLS, (i + 1) * COLS)
            return jnp.concatenate(
                [ag[p * nk + k, :, :, :, cols].reshape(rows, COLS) for p in range(PARTS)], axis=0
            )

        contract = (((0,), (0,)), ((), ()))
        hidden, d_gate, d_up = units(0), units(1), units(2)
        for n in range(4):
            cols = slice(n * 256, (n + 1) * 256)
            t = tok[:, :, :, :, cols].reshape(PARTS * rows, 256)
            for d, mask, out in ((d_gate, mg, gg), (d_up, mu, gu)):
                res = lax.dot_general(t, d, contract, preferred_element_type=F32)
                for r in range(2):
                    keep = jnp.broadcast_to(mask[k, 2 * n + r:2 * n + r + 1, :], (BLOCK, COLS))
                    kept_rows = jnp.where(keep > 0.0, res[r * BLOCK:(r + 1) * BLOCK], 0.0)
                    out[at, (2 * n + r) * BLOCK:(2 * n + r + 1) * BLOCK, :] = kept_rows.astype(BF16)
            g = grd[:, :, :, :, cols].reshape(PARTS * rows, 256)
            res = lax.dot_general(hidden, g, contract, preferred_element_type=F32)
            for i in range(blocks):
                row = md[pl.ds(blocks * k + i, 1), cols]
                keep = jnp.broadcast_to(row, (BLOCK, 256))
                kept_rows = jnp.where(keep > 0.0, res[i * BLOCK:(i + 1) * BLOCK], 0.0)
                gd[at, i * BLOCK:(i + 1) * BLOCK, cols] = kept_rows.astype(BF16)
        for copy in grad_copies(k):
            copy.start()

    lag = LAGS[-1]

    def step(t, carry):
        def run(offset, what):
            s = t - offset

            @pl.when((s >= 0) & (s < steps))
            def _():
                what(s)

        k = t - LAGS[-1] - 1 - (PARTS - 1) * nk

        @pl.when((k >= 0) & (k < nk - LATE))
        def _():
            weight_grads(k)

        for offset, what in zip(LAGS, (partials, after_pair, activate, pass_partner, pass_on, back)):
            run(offset, what)

        for p in range(PARTS - 1):
            for after, what in enumerate((tail_pair, tail_x, tail_y, tail_end)):
                @pl.when(t == (p + 1) * nk - 1 + lag + after)
                def _():
                    what(p)
        return carry

    lax.fori_loop(0, steps + lag, step, 0)
    tail_pair(PARTS - 1)
    last_send()
    for k in range(nk - LATE, nk):
        weight_grads(k)
    last_sum()

    def drain(s, carry):
        @pl.when((s > 0) & (s < steps - 1))
        def _():
            remote(ysend.at[s], yrecv.at[s], ys_sem.at[s], yr_sem.at[s], partner).wait_send()
        for i in range(3):
            z_copy(s, i).wait_send()
        for i in range(7):
            ag_copy(s, i).wait_send()
        return carry

    lax.fori_loop(0, steps, drain, 0)
    for i in range(2):
        first_copy(i).wait_send()
    for i in range(4):
        straight_copy(i).wait_send()
    for p in range(PARTS):
        for a in range(2):
            for i in range(15):
                gather_copy(p, a, i).wait_send()
        if p > 0:
            for i in range(8):
                tail_copy(p, i).wait_send()
        if p < PARTS - 1:
            for i in range(3):
                x_copy(p, i).wait_send()
            across_copy(p).wait_send()
    for i in range(7):
        last_copy(i).wait_send()
    for k in (nk - 2, nk - 1):
        for copy in grad_copies(k):
            copy.wait()


def layer(tokens, gate_w, up_w, down_w, grad_out, pat_gate, pat_up, pat_down):
    rows, width = tokens.shape
    hidden = gate_w.shape[1]
    nk = hidden // COLS
    steps = PARTS * nk
    any_, vmem = pl.BlockSpec(memory_space=pl.ANY), pl.BlockSpec(memory_space=pltpu.VMEM)
    dma, three, slot_rows = pltpu.SemaphoreType.DMA, 3 * COLS, 2 * PIECE
    small = jax.ShapeDtypeStruct((rows, width), BF16)
    whole = (PARTS, 8, 2, PIECE, width)
    return pl.pallas_call(
        functools.partial(layer_kernel, nk),
        name="layer",
        out_shape=(
            small, small,
            jax.ShapeDtypeStruct((width, hidden), BF16),
            jax.ShapeDtypeStruct((width, hidden), BF16),
            jax.ShapeDtypeStruct((hidden, width), BF16),
        ),
        in_specs=[any_] * 5 + [vmem] * 3,
        out_specs=(vmem, vmem, any_, any_, any_),
        scratch_shapes=[
            pltpu.VMEM((nk, width, COLS), BF16),
            pltpu.VMEM((nk, width, COLS), BF16),
            pltpu.VMEM((nk, COLS, width), BF16),
            pltpu.VMEM((nk, 8, COLS), F32),
            pltpu.VMEM((nk, 8, COLS), F32),
            pltpu.VMEM((hidden // BLOCK, width), F32),
            pltpu.VMEM(whole, BF16),
            pltpu.VMEM(whole, BF16),
            pltpu.VMEM((SLOTS, 4, slot_rows, three), F32),
            pltpu.VMEM((steps, 4, slot_rows, three), BF16),
            pltpu.VMEM((steps, 4, slot_rows, three), BF16),
            pltpu.VMEM((steps, 3, slot_rows, three), BF16),
            pltpu.VMEM((steps, 3, slot_rows, three), BF16),
            pltpu.VMEM((steps, 2, 4, slot_rows, three), BF16),
            pltpu.VMEM((2, 2, 16 * PIECE, width), F32),
            pltpu.VMEM((PARTS, 8, 2, PIECE, width), F32),
            pltpu.VMEM((PARTS, 3, 2, 2, PIECE, width), BF16),
            pltpu.VMEM((PARTS, 3, 2, 2, PIECE, width), BF16),
            pltpu.VMEM((PARTS, 2, PIECE, width), F32),
            pltpu.VMEM((PARTS, 2, PIECE, width), BF16),
            pltpu.VMEM((PARTS, 2, PIECE, width), BF16),
            pltpu.VMEM((2, width, COLS), BF16),
            pltpu.VMEM((2, width, COLS), BF16),
            pltpu.VMEM((2, COLS, width), BF16),
            pltpu.VMEM((7, 2, PIECE, width), BF16),
            pltpu.VMEM((7, 2, PIECE, width), BF16),
            dma((3, nk)), dma((2, PARTS)), dma((PARTS, 2, 15)), dma((PARTS, 2, 15)),
            dma((steps,)), dma((steps,)), dma((steps, 3)), dma((steps, 3)),
            dma((steps, 7)), dma((steps, 7)), dma((PARTS, 8)), dma((PARTS, 8)),
            dma((PARTS, 3)), dma((PARTS, 3)), dma((PARTS,)), dma((PARTS,)),
            dma((2, 3)), dma((7,)), dma((7,)), dma((4,)), dma((8,)),
        ],
        compiler_params=pltpu.CompilerParams(
            collective_id=0, has_side_effects=True, vmem_limit_bytes=60 * 2**20
        ),
    )(tokens, gate_w, up_w, down_w, grad_out, pat_gate, pat_up, pat_down)


def hand_out_kernel(*refs):
    n = len(refs) // 2
    for src, dst in zip(refs[:n], refs[n:]):
        dst[...] = src[...]


def hand_out(*arrays):
    def block(a):
        if a.shape[0] < 256:
            return pl.BlockSpec(a.shape, lambda i: (0, 0))
        return pl.BlockSpec((a.shape[0] // CUTS, a.shape[1]), lambda i: (i, 0))

    specs = tuple(block(a) for a in arrays)
    return pl.pallas_call(
        hand_out_kernel,
        name="hand_out",
        grid=(CUTS,),
        out_shape=tuple(jax.ShapeDtypeStruct(a.shape, a.dtype) for a in arrays),
        in_specs=list(specs),
        out_specs=specs,
        compiler_params=pltpu.CompilerParams(vmem_limit_bytes=60 * 2**20),
    )(*arrays)


def per_device(*args):
    return hand_out(*layer(*args))


def solution(mesh):
    placed = (
        P("hidden", "width"),
        P("width", "hidden"),
        P("width", "hidden"),
        P("hidden", "width"),
        P("hidden", "width"),
        P("width", None),
        P("width", None),
        P("hidden", None),
    )
    return jax.shard_map(
        per_device,
        mesh=mesh,
        in_specs=placed,
        out_specs=(
            P("hidden", "width"),
            P("hidden", "width"),
            P("width", "hidden"),
            P("width", "hidden"),
            P("hidden", "width"),
        ),
        check_vma=False,
    )
```
